32 devices in a mesh: brick: 8 (over z, y), region: 4 (over x, core).
Axes of the slice: x: 2, y: 2, z: 4, core: 2. Of those that a mesh axis runs over, the one named last changes fastest.
Arguments:
- micrograph: bfloat16 [4, 8, 512], P('region', 'brick'), may hold values from -6 to 6
- tissue: int32 [4, 8], P('region', 'brick'), may hold values from 0 to 1, as said below
- neighbours: int32 [4, 8, 26], P('region', 'brick'), may hold values from -1 to 7, as said below
- first_weight: bfloat16 [64, 27], replicated, may hold values from -1.25 to 1.25
- first_bias: float32 [64], replicated, may hold values from -3 to 3
- second_weight: bfloat16 [64, 1728], replicated, may hold values from -0.15625 to 0.15625
- second_bias: float32 [64], replicated, may hold values from -3 to 3
- head_weight: bfloat16 [4, 64], replicated, may hold values from -0.75 to 0.75
- head_bias: float32 [4], replicated, may hold values from -3 to 3
- cotangent: bfloat16 [4, 8, 4, 512], P('region', 'brick'), may hold values from -6 to 6
Outputs:
- prediction: bfloat16 [4, 8, 4, 512], P('region', 'brick')
- first_weight_grad: float32 [64, 27], replicated
- first_bias_grad: float32 [64], replicated
- second_weight_grad: float32 [64, 1728], replicated
- second_bias_grad: float32 [64], replicated
- head_weight_grad: float32 [4, 64], replicated
- head_bias_grad: float32 [4], replicated
The draws below stay inside these ranges and needn't reach their ends.
Inputs may be any that keep to these rules, and one draw needn't show every extreme that they name: 1 marks a slot that holds a tissue brick, 0 an empty slot whose outputs are zero. `neighbours`: an entry is -1 or the index, in the same region, of a tissue brick that touches the brick in that direction; empty slots list -1 only; the lists are symmetric (if brick n lists m in direction (a, b, c), m lists n in direction (-a, -b, -c)); every entry in a direction with b ≠ 0 is -1 (a region is one brick thick along y); a brick m listed by n in direction (a, 0, c) has m = n + 2 a + c, so its device is at most 3 away, and in every draw some brick lists one whose device is exactly 3 away.
All inputs are finite; a program needn't handle non-finite values.
Results may differ from the reference program's by a relative error of at most 0.015.
Values may be sent and summed in bfloat16 or wider, within the bound.
A program may use at most 64 MiB of HBM per device.

```python
from functools import partial
import jax
import jax.numpy as jnp
from jax import lax

C = 64
OUT_CH = 4
EDGE = 8
TAPS = 27
BRICKS_DEV = 1
CELLS = 512
BRICKS = 8
REGIONS = 4


DIRECTIONS = [(shift_x, shift_y, shift_z) for shift_x in (-1, 0, 1) for shift_y in (-1, 0, 1) for shift_z in (-1, 0, 1) if (shift_x, shift_y, shift_z) != (0, 0, 0)]


def tissue_layout(key):
    chosen = jax.random.randint(key, (REGIONS, BRICKS), 0, 4)
    slot_ids = jnp.arange(BRICKS, dtype=jnp.int32)
    column = slot_ids // BRICKS_DEV // 2
    filled = jnp.where(chosen > 0, 1, 0)
    return jnp.where(column[None, :] < 2, 1, filled).astype(jnp.int32)


def draw_tissue(key, part):
    present = tissue_layout(key)
    key = jax.random.fold_in(key, 5)
    return present


def draw_neighbours(key, part):
    present = tissue_layout(key)
    key = jax.random.fold_in(key, 7)
    slot_ids = jnp.arange(BRICKS, dtype=jnp.int32)
    across = slot_ids % BRICKS_DEV
    device_ids = slot_ids // BRICKS_DEV
    layer = device_ids % 2
    column = device_ids // 2
    columns_all = BRICKS // BRICKS_DEV // 2
    lists = []
    for shift_x, shift_y, shift_z in DIRECTIONS:
        new_column = column + shift_x
        new_across = across + shift_y
        new_layer = layer + shift_z
        inside = (new_column >= 0) & (new_column < columns_all) & (new_across >= 0) & (new_across < BRICKS_DEV) & (new_layer >= 0) & (new_layer < 2)
        target = jnp.clip(BRICKS_DEV * (2 * new_column + new_layer) + new_across, 0, BRICKS - 1).astype(jnp.int32)
        linked = inside[None, :] & (present == 1) & (jnp.take(present, target, axis=1) == 1)
        lists.append(jnp.where(linked, target[None, :], -1))
    return jnp.stack(lists, axis=-1).astype(jnp.int32)


def level_of(key, shape, cuts, low, largest):
    def one(dim, shards_of):
        heights = jax.random.uniform(jax.random.fold_in(jax.random.fold_in(key, 6), dim), (shards_of,), jnp.float32, low / len(cuts), largest / len(cuts))
        return jnp.repeat(jnp.exp(heights), shape[dim] // shards_of).reshape((-1,) + (1,) * (len(shape) - dim - 1))

    level = one(*cuts[0])
    for cut in cuts[1:]:
        level = level * one(*cut)
    return level


def centred(stream_key, dims, spread, most, split=(), kind=jnp.bfloat16):
    entries = jax.random.normal(stream_key, dims, jnp.float32) * spread
    if len(split) > 0:
        entries = level_of(stream_key, dims, split, -0.22, 0.18) * entries
    return jnp.clip(entries, min=-most, max=most).astype(kind)


def setup_inputs(seed: int = 0) -> dict:
    keys = jax.random.split(jax.random.key(seed), 11)
    return {
        "micrograph": centred(keys[0], (REGIONS, BRICKS, CELLS), 1.0, 6.0, ((0, 4), (1, 8))),
        "tissue": draw_tissue(jax.random.fold_in(keys[10], 71), 0),
        "neighbours": draw_neighbours(jax.random.fold_in(keys[10], 71), 0),
        "first_weight": centred(keys[3], (C, TAPS), TAPS ** -0.5, 1.25),
        "first_bias": centred(keys[4], (C,), 0.5, 3.0, (), jnp.float32),
        "second_weight": centred(keys[5], (C, TAPS * C), (TAPS * C) ** -0.5, 0.15625),
        "second_bias": centred(keys[6], (C,), 0.5, 3.0, (), jnp.float32),
        "head_weight": centred(keys[7], (OUT_CH, C), C ** -0.5, 0.75),
        "head_bias": centred(keys[8], (OUT_CH,), 0.5, 3.0, (), jnp.float32),
        "cotangent": centred(keys[9], (REGIONS, BRICKS, OUT_CH, CELLS), 1.0, 6.0, ((0, 4), (1, 8))),
    }


DIRECTIONS = [(shift_x, shift_y, shift_z) for shift_x in (-1, 0, 1) for shift_y in (-1, 0, 1) for shift_z in (-1, 0, 1) if (shift_x, shift_y, shift_z) != (0, 0, 0)]
TAP_OFFSETS = [(shift_x, shift_y, shift_z) for shift_x in (-1, 0, 1) for shift_y in (-1, 0, 1) for shift_z in (-1, 0, 1)]

def face_table(volume, margin):
    side_len = volume.shape[-1]
    sections = [volume[:, :, :margin], volume[:, :, side_len - margin:], volume[:, :, :, :margin], volume[:, :, :, side_len - margin:], volume[:, :, :, :, :margin], volume[:, :, :, :, side_len - margin:]]
    return jnp.concatenate([section.reshape(section.shape[0], section.shape[1], -1) for section in sections], axis=2)

def assemble(volume, table, row_index, present, margin):
    number, channels, side_len = (volume.shape[0], volume.shape[1], volume.shape[2])
    face_size = margin * side_len * side_len
    padded = jnp.pad(volume, ((0, 0), (0, 0), (margin, margin), (margin, margin), (margin, margin)))
    for dir_index, direction in enumerate(DIRECTIONS):
        normal = [axis_id for axis_id in range(3) if direction[axis_id] != 0][0]
        face_index = 2 * normal + (0 if direction[normal] > 0 else 1)
        selected = jnp.take(table[:, :, face_index * face_size:(face_index + 1) * face_size], row_index[:, dir_index], axis=0)
        extent = [side_len, side_len, side_len]
        extent[normal] = margin
        selected = selected.reshape((number, channels) + tuple(extent))
        sources = []
        targets = []
        for axis_id in range(3):
            if axis_id == normal or direction[axis_id] > 0:
                sources.append(slice(0, margin))
            elif direction[axis_id] < 0:
                sources.append(slice(side_len - margin, side_len))
            else:
                sources.append(slice(0, side_len))
            if direction[axis_id] > 0:
                targets.append(slice(side_len + margin, side_len + 2 * margin))
            elif direction[axis_id] < 0:
                targets.append(slice(0, margin))
            else:
                targets.append(slice(margin, margin + side_len))
        portion = selected[:, :, sources[0], sources[1], sources[2]]
        presence = present[:, dir_index].astype(portion.dtype).reshape(number, 1, 1, 1, 1)
        padded = padded.at[:, :, targets[0], targets[1], targets[2]].set(portion * presence)
    return padded

def convolve(padded, blocks, margin, out_len, sign):
    number, inputs = (padded.shape[0], padded.shape[1])
    running = None
    for tap_index, offset in enumerate(TAP_OFFSETS):
        start_x, start_y, start_z = [margin + sign * value for value in offset]
        window_view = padded[:, :, start_x:start_x + out_len, start_y:start_y + out_len, start_z:start_z + out_len].reshape(number, inputs, -1)
        contrib = jnp.einsum('oi,nip->nop', blocks[tap_index].astype(jnp.float32), window_view.astype(jnp.float32))
        running = contrib if running is None else running + contrib
    return running

def tap_grads(left, padded, margin, out_len, exact):
    number, inputs = (padded.shape[0], padded.shape[1])
    columns = []
    for offset in TAP_OFFSETS:
        start_x, start_y, start_z = [margin + value for value in offset]
        window_view = padded[:, :, start_x:start_x + out_len, start_y:start_y + out_len, start_z:start_z + out_len].reshape(number, inputs, -1)
        if exact:
            columns.append(jnp.einsum('nop,nip->oi', left.astype(jnp.float32), window_view.astype(jnp.float32), precision=lax.Precision.HIGHEST))
        else:
            columns.append(jnp.einsum('nop,nip->oi', left.astype(jnp.float32), window_view.astype(jnp.float32)))
    return jnp.concatenate(columns, axis=1)

def gelu_slope(values):
    _, backward = jax.vjp(partial(jax.nn.gelu, approximate=True), values)
    return backward(jnp.ones_like(values))[0]

def reference(micrograph, tissue, neighbours, first_weight, first_bias, second_weight, second_bias, head_weight, head_bias, cotangent):
    channels = first_weight.shape[0]
    blocks_first = first_weight.astype(jnp.float32).T[:, :, None]
    blocks_second = second_weight.astype(jnp.float32).reshape(channels, TAPS, channels).transpose(1, 0, 2)
    blocks_back = blocks_second.transpose(0, 2, 1)
    head_f = head_weight.astype(jnp.float32)
    grad_w1 = jnp.zeros((channels, TAPS), jnp.float32)
    grad_b1 = jnp.zeros((channels,), jnp.float32)
    grad_w2 = jnp.zeros((channels, TAPS * channels), jnp.float32)
    grad_b2 = jnp.zeros((channels,), jnp.float32)
    grad_wh = jnp.zeros((OUT_CH, channels), jnp.float32)
    grad_bh = jnp.zeros((OUT_CH,), jnp.float32)
    outputs = []
    for region_id in range(REGIONS):
        active = tissue[region_id].astype(jnp.float32).reshape(BRICKS, 1, 1)
        row_index = jnp.maximum(neighbours[region_id], 0).astype(jnp.int32)
        present = neighbours[region_id] >= 0
        volume = micrograph[region_id].reshape(BRICKS, 1, EDGE, EDGE, EDGE)
        em_pad = assemble(volume, face_table(volume, 1), row_index, present, 1)
        z_first = convolve(em_pad, blocks_first, 1, EDGE, 1) + first_bias[None, :, None]
        h_first = (jax.nn.gelu(z_first, approximate=True) * active).astype(jnp.bfloat16)
        cube_first = h_first.reshape(BRICKS, channels, EDGE, EDGE, EDGE)
        first_pad = assemble(cube_first, face_table(cube_first, 1), row_index, present, 1)
        z_second = convolve(first_pad, blocks_second, 1, EDGE, 1) + second_bias[None, :, None]
        h_second = (jax.nn.gelu(z_second, approximate=True) * active).astype(jnp.bfloat16)
        linear = jnp.einsum('kc,ncp->nkp', head_f, h_second.astype(jnp.float32)) + head_bias[None, :, None]
        outputs.append((linear * active).astype(jnp.bfloat16))
        dpred = (cotangent[region_id].astype(jnp.float32) * active / (BRICKS * REGIONS)).astype(jnp.bfloat16)
        grad_wh = grad_wh + jnp.einsum('nkp,ncp->kc', dpred.astype(jnp.float32), h_second.astype(jnp.float32))
        grad_bh = grad_bh + lax.optimization_barrier(jnp.sum(dpred.astype(jnp.float32), axis=(0, 2)))
        dh_second = jnp.einsum('kc,nkp->ncp', head_f, dpred.astype(jnp.float32))
        dz_second = (dh_second * gelu_slope(z_second) * active).astype(jnp.bfloat16)
        grad_w2 = grad_w2 + tap_grads(dz_second, first_pad, 1, EDGE, False)
        grad_b2 = grad_b2 + lax.optimization_barrier(jnp.sum(dz_second.astype(jnp.float32), axis=(0, 2)))
        cube_grad = dz_second.reshape(BRICKS, channels, EDGE, EDGE, EDGE)
        grad_pad = assemble(cube_grad, face_table(cube_grad, 1), row_index, present, 1)
        dh_first = convolve(grad_pad, blocks_back, 1, EDGE, -1)
        dz_first = dh_first * gelu_slope(z_first) * active
        grad_w1 = grad_w1 + tap_grads(dz_first, em_pad, 1, EDGE, True)
        grad_b1 = grad_b1 + lax.optimization_barrier(jnp.sum(dz_first, axis=(0, 2)))
    prediction = jnp.stack(outputs, axis=0)
    return (prediction, grad_w1, grad_b1, grad_w2, grad_b2, grad_wh, grad_bh)
```

```python
import functools
import math

import jax
import jax.numpy as jnp
from jax import lax
from jax.experimental import pallas as pl
from jax.experimental.pallas import tpu as pltpu
from jax.sharding import PartitionSpec as P

F32 = jnp.float32
BF16 = jnp.bfloat16
MESH = pl.DeviceIdType.MESH
TAPS = 27
PLANE = 64
CELLS = 512
WIDE = 640
DELTAS = (-3, -2, -1, 1, 2, 3)
CHUNKS = 8
CHUNK = 256
MAIN = 7 * CHUNK
MIC_ROWS = 32
SLOPE = math.sqrt(2 / math.pi)
CUBIC = 0.044715


def direction_id(a, c):
    full = (a + 1) * 9 + 3 + (c + 1)
    return full if full < 13 else full - 1


def iota(shape, dim):
    return lax.broadcasted_iota(jnp.int32, shape, dim)


def dot(left, right):
    return lax.dot_general(left, right, (((1,), (0,)), ((), ())), preferred_element_type=F32)


def dot_nt(left, right):
    return lax.dot_general(left, right, (((1,), (1,)), ((), ())), preferred_element_type=F32)


def column(row):
    size = row.shape[1]
    wide = jnp.broadcast_to(row, (size, size))
    return jnp.sum(jnp.where(iota((size, size), 0) == iota((size, size), 1), wide, 0.0), axis=1, keepdims=True)


def gelu_parts(values):
    square = values * values
    bent = jnp.tanh(SLOPE * (values + CUBIC * square * values))
    half = 0.5 * (1.0 + bent)
    slope = half + 0.5 * values * (1.0 - bent * bent) * (SLOPE * (1.0 + 3.0 * CUBIC * square))
    return values * half, slope


def halves(values):
    high = values.astype(BF16)
    return jnp.concatenate([high, (values - high.astype(F32)).astype(BF16)], axis=1)


def joined(pair):
    return pair[:, :128].astype(F32) + pair[:, 128:].astype(F32)


def for_each(count, body):
    if count <= 8:
        for step in range(count):
            body(step)
    else:
        def step_body(step, carry):
            body(step)
            return carry

        lax.fori_loop(0, count, step_body, 0)


def pack(field, pick, packet):
    rows = field.shape[0]
    low = iota((rows, 128), 1) < PLANE
    packet[0] = dot(field.astype(BF16), pick).astype(BF16)
    packet[1] = jnp.where(low, field[:, :128], field[:, CELLS - 128 :]).astype(BF16)


def widen(field, box, flags, spread):
    rows = field.shape[0]
    lane = iota((rows, 128), 1)
    m3, m2, m1, p1, p2, p3 = [box[k].astype(F32) for k in range(6)]
    ends = jnp.where(lane < PLANE, p2 * flags[1, 0], m2 * flags[-1, 0])
    padded = pltpu.roll(jnp.concatenate([field, ends], axis=1), 64, 1)
    first, inner, last = lane < 8, lane < 72, lane < 80
    above = jnp.where(
        first,
        pltpu.roll(m1, 72, 1) * flags[-1, 1],
        jnp.where(
            inner,
            pltpu.roll(p1, 8, 1) * flags[0, 1],
            jnp.where(last, pltpu.roll(p3, 72, 1) * flags[1, 1], 0.0),
        ),
    )
    below = jnp.where(
        first,
        pltpu.roll(m3, 8, 1) * flags[-1, -1],
        jnp.where(
            inner,
            pltpu.roll(m1, 72, 1) * flags[0, -1],
            jnp.where(last, pltpu.roll(p1, 8, 1) * flags[1, -1], 0.0),
        ),
    )
    halo = dot(jnp.concatenate([above, below], axis=1).astype(BF16), spread)
    return padded, halo


def windows(padded, halo, emit):
    lane = iota(padded.shape, 1)
    z = lane % 8
    y = (lane // 8) % 8
    for c in (-1, 0, 1):
        if c == 0:
            along = padded
        elif c == 1:
            along = jnp.where(z == 7, halo, pltpu.roll(padded, WIDE - 1, 1))
        else:
            along = jnp.where(z == 0, halo, pltpu.roll(padded, 1, 1))
        emit(3 + c + 1, along)
        emit(c + 1, jnp.where(y == 0, 0.0, pltpu.roll(along, 8, 1)))
        emit(6 + c + 1, jnp.where(y == 7, 0.0, pltpu.roll(along, WIDE - 8, 1)))


def kernel(
    nb,
    nr,
    total_bricks,
    mic_ref,
    tis_ref,
    nei_ref,
    w1_ref,
    b1_ref,
    w2_ref,
    b2_ref,
    hw_ref,
    hb_ref,
    cot_ref,
    pred_ref,
    gw1_ref,
    gb1_ref,
    gw2_ref,
    gb2_ref,
    gwh_ref,
    gbh_ref,
    s1_ref,
    s2_ref,
    w1p_ref,
    w2p_ref,
    back_ref,
    a_ref,
    pick_ref,
    spread_ref,
    mic_out,
    h1_out,
    dz_out,
    mic_box,
    h1_box,
    dz_box,
    grad_ref,
    ra_ref,
    rb_src,
    rb_ref,
    fin_ref,
    ex_send,
    ex_recv,
    a_send,
    a_recv,
    b_send,
    b_recv,
    gb_send,
    gb_recv,
    ga_send,
    ga_recv,
):
    me = lax.axis_index("brick")
    mr = lax.axis_index("region")
    channels = w2_ref.shape[0]
    rows = channels // nr

    for box in (mic_box, h1_box, dz_box):
        box[...] = jnp.zeros_like(box)

    barrier = pltpu.get_barrier_semaphore()

    def greet_brick(step):
        pl.semaphore_signal(
            barrier, inc=1, device_id={"brick": (me + 1 + step) % nb}, device_id_type=MESH
        )

    for_each(nb - 1, greet_brick)
    for step in range(nr - 1):
        pl.semaphore_signal(
            barrier, inc=1, device_id={"region": (mr + 1 + step) % nr}, device_id_type=MESH
        )

    spot, slot = iota((CELLS, 128), 0), iota((CELLS, 128), 1)
    pick_ref[...] = jnp.where(
        spot == (slot % PLANE) * 8 + 7 * (slot // PLANE), 1.0, 0.0
    ).astype(BF16)
    pick = pick_ref[...]
    mic = jnp.broadcast_to(mic_ref[...].astype(F32), (MIC_ROWS, CELLS))
    pack(mic, pick, mic_out)

    def exchange(index, packet, box, act):
        for k, delta in enumerate(DELTAS):
            back = DELTAS.index(-delta)
            other = me + delta

            @pl.when((other >= 0) & (other < nb))
            def _():
                if act == "recv":
                    copy = pltpu.make_async_remote_copy(
                        src_ref=packet.at[1 if abs(delta) == 2 else 0],
                        dst_ref=box.at[k],
                        send_sem=ex_send.at[index, k],
                        recv_sem=ex_recv.at[index, k],
                        device_id={"brick": other},
                        device_id_type=MESH,
                    )
                    copy.wait_recv()
                else:
                    copy = pltpu.make_async_remote_copy(
                        src_ref=packet.at[1 if abs(delta) == 2 else 0],
                        dst_ref=box.at[back],
                        send_sem=ex_send.at[index, k],
                        recv_sem=ex_recv.at[index, back],
                        device_id={"brick": other},
                        device_id_type=MESH,
                    )
                    if act == "start":
                        copy.start()
                    else:
                        copy.wait_send()

    pl.semaphore_wait(barrier, nb - 1 + nr - 1)
    exchange(0, mic_out, mic_box, "start")

    spread_row, spread_lane = iota((256, WIDE), 0), iota((256, WIDE), 1)
    spread_ref[...] = jnp.where(
        spread_lane == (spread_row % 128) * 8 + 7 * (1 - spread_row // 128), 1.0, 0.0
    ).astype(BF16)
    w1p_ref[...] = jnp.zeros_like(w1p_ref)
    w1p_ref[:, :TAPS] = w1_ref[...]
    w2p_ref[:, MAIN - 128 :] = jnp.zeros((channels, 128), BF16)
    w2p_ref[:, : TAPS * channels] = w2_ref[...]
    s1_ref[TAPS * channels :, :] = jnp.zeros((channels, CELLS), BF16)
    s2_ref[TAPS * channels :, :] = jnp.zeros((channels, CELLS), BF16)
    for j in range(14):
        upper = w2p_ref[:, 128 * (13 - j) : 128 * (14 - j)].astype(F32)
        if j < 13:
            lower = w2p_ref[:, 128 * (12 - j) : 128 * (13 - j)].astype(F32)
        else:
            lower = jnp.zeros((channels, 128), F32)
        turned = jnp.concatenate([upper, lower], axis=0).T
        back_ref[:, 128 * j : 128 * (j + 1)] = jnp.where(
            iota((channels, 128), 1) < channels, turned[:channels], turned[channels:]
        ).astype(BF16)
    flags = {}
    for a in (-1, 0, 1):
        for c in (-1, 0, 1):
            if (a, c) != (0, 0):
                flags[a, c] = jnp.where(nei_ref[0, direction_id(a, c)] >= 0, 1.0, 0.0).astype(F32)
    active = tis_ref[0, 0].astype(F32)
    bias1 = column(b1_ref[...])
    bias2 = column(b2_ref[...])
    bias3 = jnp.sum(
        jnp.where(iota((4, 4), 0) == iota((4, 4), 1), jnp.broadcast_to(hb_ref[...], (4, 4)), 0.0),
        axis=1,
        keepdims=True,
    )
    dpred = (cot_ref[...].astype(F32) * active / total_bricks).astype(BF16)
    dpred_wide = jnp.concatenate([dpred.astype(F32), jnp.zeros((4, CELLS), F32)], axis=0)
    d_second = lax.dot_general(
        hw_ref[...], dpred, (((0,), (0,)), ((), ())), preferred_element_type=F32
    )

    exchange(0, mic_out, mic_box, "recv")
    spread = spread_ref[...]
    padded, halo = widen(mic, mic_box, flags, spread)
    row = iota((MIC_ROWS, CELLS), 0)
    taps = [jnp.where((row >= 27) & (row < 30), 1.0, 0.0).astype(F32)]

    def emit_mic(index, value):
        rolled = pltpu.roll(value, WIDE - PLANE, 1)
        views = (value[:, :CELLS], rolled[:, :CELLS], value[:, 128:])
        for a in range(3):
            taps[0] = jnp.where(row == 9 * a + index, views[a], taps[0])

    windows(padded, halo, emit_mic)
    a_ref[...] = jnp.concatenate(
        [taps[0], dpred_wide, jnp.zeros((128 - MIC_ROWS - 8, CELLS), F32)], axis=0
    ).astype(BF16)
    z1 = dot(w1p_ref[...], a_ref[...]) + bias1
    value1, slope1 = gelu_parts(z1)
    h1 = (value1 * active).astype(BF16).astype(F32)
    pack(h1, pick, h1_out)
    exchange(1, h1_out, h1_box, "start")
    slope1 = slope1 * active

    def store_windows(target):
        def emit(index, value):
            rolled = pltpu.roll(value, WIDE - PLANE, 1)
            views = (value[:, :CELLS], rolled[:, :CELLS], value[:, 128:])
            for a in range(3):
                start = (9 * a + index) * channels
                target[start : start + channels, :] = views[a].astype(BF16)

        return emit

    exchange(1, h1_out, h1_box, "recv")
    padded, halo = widen(h1, h1_box, flags, spread)
    windows(padded, halo, store_windows(s1_ref))
    z2 = dot(w2p_ref[...], s1_ref[...]) + bias2
    value2, slope2 = gelu_parts(z2)
    dz2 = (d_second * slope2 * active).astype(BF16)
    pack(dz2.astype(F32), pick, dz_out)
    exchange(2, dz_out, dz_box, "start")

    grad_ref[:, :MAIN] = dot_nt(dz2, s1_ref[...]).astype(BF16)

    def region_copy(part, step, act):
        other = (mr + 1 + step) % nr
        lanes = pl.ds(0, MAIN) if part == 0 else pl.ds(MAIN, CHUNK)
        owner = other if act != "recv" else mr
        slot_id = mr if act != "recv" else other
        copy = pltpu.make_async_remote_copy(
            src_ref=grad_ref.at[pl.ds(pl.multiple_of(owner * rows, rows), rows), lanes],
            dst_ref=ra_ref.at[slot_id, :, lanes],
            send_sem=a_send.at[part, other],
            recv_sem=a_recv.at[part, slot_id],
            device_id={"region": other},
            device_id_type=MESH,
        )
        if act == "start":
            copy.start()
        elif act == "recv":
            copy.wait_recv()
        else:
            copy.wait_send()

    for step in range(nr - 1):
        region_copy(0, step, "start")

    h2 = (value2 * active).astype(BF16)
    linear = dot(hw_ref[...], h2) + bias3
    pred_ref[...] = (linear * active).astype(BF16)
    tap_rows = a_ref[...]
    dpred_tall = jnp.concatenate(
        [dpred_wide, jnp.zeros((channels - 8, CELLS), F32)], axis=0
    ).astype(BF16)
    lane = iota((channels, 128), 1)
    small = jnp.where(lane == 28, dot_nt(dz2, tap_rows), 0.0)
    small = small + jnp.where((lane >= 32) & (lane < 36), dot_nt(h2, tap_rows), 0.0)
    small = small + jnp.where(lane == 29, dot_nt(dpred_tall, tap_rows), 0.0)

    exchange(2, dz_out, dz_box, "recv")
    padded, halo = widen(dz2.astype(F32), dz_box, flags, spread)
    windows(padded, halo, store_windows(s2_ref))
    dz1 = (dot(back_ref[...], s2_ref[...]) * slope1).astype(BF16)
    small = small + jnp.where(lane < 28, dot_nt(dz1, tap_rows), 0.0)
    grad_ref[:, MAIN:] = halves(small)
    for step in range(nr - 1):
        region_copy(1, step, "start")

    def brick_copy(chunk, act):
        @pl.when(me != chunk)
        def _():
            copy = pltpu.make_async_remote_copy(
                src_ref=rb_src.at[chunk],
                dst_ref=rb_ref.at[me],
                send_sem=b_send.at[chunk],
                recv_sem=b_recv.at[me],
                device_id={"brick": chunk},
                device_id_type=MESH,
            )
            if act == "start":
                copy.start()
            else:
                copy.wait_send()

    mine = pl.ds(pl.multiple_of(mr * rows, rows), rows)

    def region_sum(part):
        lanes = pl.ds(0, MAIN) if part == 0 else pl.ds(MAIN, CHUNK)
        for step in range(nr - 1):
            region_copy(part, step, "recv")
        total = grad_ref[mine, lanes].astype(F32)
        for step in range(nr - 1):
            total = total + ra_ref[(mr + 1 + step) % nr, :, lanes].astype(F32)
        return total

    total = region_sum(0)
    for chunk in range(CHUNKS - 1):
        rb_src[chunk] = total[:, CHUNK * chunk : CHUNK * (chunk + 1)].astype(BF16)
        brick_copy(chunk, "start")
    rb_src[CHUNKS - 1] = halves(joined(region_sum(1)))
    brick_copy(CHUNKS - 1, "start")

    def gather_copy(step, act):
        other = (me + 1 + step) % nb
        copy = pltpu.make_async_remote_copy(
            src_ref=fin_ref.at[mr, me % CHUNKS],
            dst_ref=fin_ref.at[mr, me % CHUNKS],
            send_sem=gb_send.at[other],
            recv_sem=gb_recv.at[me % CHUNKS],
            device_id={"brick": other},
            device_id_type=MESH,
        )
        if act == "start":
            copy.start()
        else:
            copy.wait_send()

    def own():
        def arrived(step):
            other = (me + 1 + step) % nb
            pltpu.make_async_remote_copy(
                src_ref=rb_src.at[0],
                dst_ref=rb_ref.at[other],
                send_sem=b_send.at[0],
                recv_sem=b_recv.at[other],
                device_id={"brick": other},
                device_id_type=MESH,
            ).wait_recv()

        for_each(nb - 1, arrived)
        kept = rb_src[me % CHUNKS].astype(F32)
        if nb <= CHUNKS:
            for step in range(nb - 1):
                kept = kept + rb_ref[(me + 1 + step) % nb].astype(F32)
        else:
            kept = lax.fori_loop(
                0, nb - 1, lambda step, s: s + rb_ref[(me + 1 + step) % nb].astype(F32), kept
            )
        fin_ref[mr, me % CHUNKS] = jnp.where(me == CHUNKS - 1, halves(joined(kept)), kept.astype(BF16))
        for_each(nb - 1, lambda step: gather_copy(step, "start"))

    if nb > CHUNKS:
        pl.when(me < CHUNKS)(own)
    else:
        own()

    for chunk in range(CHUNKS):
        @pl.when(me != chunk)
        def _():
            pltpu.make_async_remote_copy(
                src_ref=fin_ref.at[mr, chunk],
                dst_ref=fin_ref.at[mr, chunk],
                send_sem=gb_send.at[chunk],
                recv_sem=gb_recv.at[chunk],
                device_id={"brick": chunk},
                device_id_type=MESH,
            ).wait_recv()

    def spread_copy(step, act):
        other = (mr + 1 + step) % nr
        slot_id = other if act == "recv" else mr
        copy = pltpu.make_async_remote_copy(
            src_ref=fin_ref.at[slot_id],
            dst_ref=fin_ref.at[slot_id],
            send_sem=ga_send.at[other],
            recv_sem=ga_recv.at[slot_id],
            device_id={"region": other},
            device_id_type=MESH,
        )
        if act == "start":
            copy.start()
        elif act == "recv":
            copy.wait_recv()
        else:
            copy.wait_send()

    for step in range(nr - 1):
        spread_copy(step, "start")
    exchange(0, mic_out, mic_box, "sent")
    exchange(1, h1_out, h1_box, "sent")
    exchange(2, dz_out, dz_box, "sent")
    for part in range(2):
        for step in range(nr - 1):
            region_copy(part, step, "sent")
    for chunk in range(CHUNKS):
        brick_copy(chunk, "sent")
    if nb > CHUNKS:
        pl.when(me < CHUNKS)(lambda: for_each(nb - 1, lambda step: gather_copy(step, "sent")))
    else:
        for_each(nb - 1, lambda step: gather_copy(step, "sent"))
    for step in range(nr - 1):
        spread_copy(step, "recv")
    for region in range(nr):
        where = slice(region * rows, (region + 1) * rows)
        for chunk in range(CHUNKS - 1):
            block = fin_ref[region, chunk].astype(F32)
            if chunk < CHUNKS - 2:
                gw2_ref[where, CHUNK * chunk : CHUNK * (chunk + 1)] = block
            else:
                gw2_ref[where, CHUNK * chunk : CHUNK * chunk + 128] = block[:, :128]
                gw2_ref[where, CHUNK * chunk + 128 : TAPS * channels] = block[
                    :, 128 : TAPS * channels - CHUNK * chunk
                ]
    small = jnp.concatenate(
        [joined(fin_ref[region, CHUNKS - 1]) for region in range(nr)], axis=0
    )
    gw1_ref[...] = small[:, :TAPS]
    turned = jnp.concatenate([small, jnp.zeros((128 - channels, 128), F32)], axis=0).T
    gb1_ref[...] = turned[27:28, :channels]
    gb2_ref[...] = turned[28:29, :channels]
    gbh_ref[...] = turned[29:30, :4]
    gwh_ref[...] = turned[32:36, :channels]
    for step in range(nr - 1):
        spread_copy(step, "sent")


def solution(mesh):
    nb, nr = mesh.shape["brick"], mesh.shape["region"]

    def shards(mic, tissue, neighbours, w1, b1, w2, b2, hw, hb, cot):
        channels = w1.shape[0]
        rows = channels // nr
        vmem = pl.BlockSpec(memory_space=pltpu.VMEM)
        smem = pl.BlockSpec(memory_space=pltpu.SMEM)
        dma = pltpu.SemaphoreType.DMA
        total_bricks = nb * nr * mic.shape[1]
        outs = pl.pallas_call(
            functools.partial(kernel, nb, nr, total_bricks),
            out_shape=(
                jax.ShapeDtypeStruct((4, CELLS), BF16),
                jax.ShapeDtypeStruct((channels, TAPS), F32),
                jax.ShapeDtypeStruct((1, channels), F32),
                jax.ShapeDtypeStruct((channels, TAPS * channels), F32),
                jax.ShapeDtypeStruct((1, channels), F32),
                jax.ShapeDtypeStruct((4, channels), F32),
                jax.ShapeDtypeStruct((1, 4), F32),
            ),
            in_specs=[vmem, smem, smem] + [vmem] * 7,
            out_specs=(vmem,) * 7,
            scratch_shapes=[
                pltpu.VMEM((MAIN, CELLS), BF16),
                pltpu.VMEM((MAIN, CELLS), BF16),
                pltpu.VMEM((channels, 128), BF16),
                pltpu.VMEM((channels, MAIN), BF16),
                pltpu.VMEM((channels, MAIN), BF16),
                pltpu.VMEM((128, CELLS), BF16),
                pltpu.VMEM((CELLS, 128), BF16),
                pltpu.VMEM((256, WIDE), BF16),
                pltpu.VMEM((2, MIC_ROWS, 128), BF16),
                pltpu.VMEM((2, channels, 128), BF16),
                pltpu.VMEM((2, channels, 128), BF16),
                pltpu.VMEM((6, MIC_ROWS, 128), BF16),
                pltpu.VMEM((6, channels, 128), BF16),
                pltpu.VMEM((6, channels, 128), BF16),
                pltpu.VMEM((channels, MAIN + CHUNK), BF16),
                pltpu.VMEM((nr, rows, MAIN + CHUNK), BF16),
                pltpu.VMEM((CHUNKS, rows, CHUNK), BF16),
                pltpu.VMEM((nb, rows, CHUNK), BF16),
                pltpu.VMEM((nr, CHUNKS, rows, CHUNK), BF16),
                dma((3, 6)),
                dma((3, 6)),
                dma((2, nr)),
                dma((2, nr)),
                dma((CHUNKS,)),
                dma((nb,)),
                dma((nb,)),
                dma((CHUNKS,)),
                dma((nr,)),
                dma((nr,)),
            ],
            compiler_params=pltpu.CompilerParams(
                collective_id=0, has_side_effects=True, vmem_limit_bytes=40 * 1024 * 1024
            ),
            cost_estimate=pl.CostEstimate(flops=360_000_000, bytes_accessed=2_000_000, transcendentals=65536),
        )(
            mic.reshape(1, CELLS),
            tissue,
            neighbours.reshape(1, 26),
            w1,
            b1.reshape(1, channels),
            w2,
            b2.reshape(1, channels),
            hw,
            hb.reshape(1, 4),
            cot.reshape(4, CELLS),
        )
        pred, gw1, gb1, gw2, gb2, gwh, gbh = outs
        return (
            pred.reshape(1, 1, 4, CELLS),
            gw1,
            gb1.reshape(channels),
            gw2,
            gb2.reshape(channels),
            gwh,
            gbh.reshape(4),
        )

    return jax.shard_map(
        shards,
        mesh=mesh,
        in_specs=(
            P("region", "brick", None),
            P("region", "brick"),
            P("region", "brick", None),
            P(),
            P(),
            P(),
            P(),
            P(),
            P(),
            P("region", "brick", None, None),
        ),
        out_specs=(P("region", "brick", None, None), P(), P(), P(), P(), P(), P()),
        check_vma=False,
    )
```

```python
import functools
import math

import jax
import jax.numpy as jnp
from jax import lax
from jax.experimental import pallas as pl
from jax.experimental.pallas import tpu as pltpu
from jax.sharding import PartitionSpec as P

F32 = jnp.float32
BF16 = jnp.bfloat16
MESH = pl.DeviceIdType.MESH
TAPS = 27
PLANE = 64
CELLS = 512
WIDE = 640
DELTAS = (-3, -2, -1, 1, 2, 3)
CHUNKS = 8
CHUNK = 256
MAIN = 7 * CHUNK
MIC_ROWS = 32
SLOPE = math.sqrt(2 / math.pi)
CUBIC = 0.044715


def direction_id(a, c):
    full = (a + 1) * 9 + 3 + (c + 1)
    return full if full < 13 else full - 1


def iota(shape, dim):
    return lax.broadcasted_iota(jnp.int32, shape, dim)


def dot(left, right):
    return lax.dot_general(left, right, (((1,), (0,)), ((), ())), preferred_element_type=F32)


def dot_nt(left, right):
    return lax.dot_general(left, right, (((1,), (1,)), ((), ())), preferred_element_type=F32)


def column(row):
    size = row.shape[1]
    wide = jnp.broadcast_to(row, (size, size))
    return jnp.sum(jnp.where(iota((size, size), 0) == iota((size, size), 1), wide, 0.0), axis=1, keepdims=True)


def gelu_parts(values):
    square = values * values
    bent = jnp.tanh(SLOPE * (values + CUBIC * square * values))
    half = 0.5 * (1.0 + bent)
    slope = half + 0.5 * values * (1.0 - bent * bent) * (SLOPE * (1.0 + 3.0 * CUBIC * square))
    return values * half, slope


def halves(values):
    high = values.astype(BF16)
    return jnp.concatenate([high, (values - high.astype(F32)).astype(BF16)], axis=1)


def joined(pair):
    return pair[:, :128].astype(F32) + pair[:, 128:].astype(F32)


def for_each(count, body):
    if count <= 8:
        for step in range(count):
            body(step)
    else:
        def step_body(step, carry):
            body(step)
            return carry

        lax.fori_loop(0, count, step_body, 0)


def pack(field, pick, packet):
    rows = field.shape[0]
    low = iota((rows, 128), 1) < PLANE
    packet[0] = dot(field.astype(BF16), pick).astype(BF16)
    packet[1] = jnp.where(low, field[:, :128], field[:, CELLS - 128 :]).astype(BF16)


def widen(field, box, flags, spread):
    rows = field.shape[0]
    lane = iota((rows, 128), 1)
    m3, m2, m1, p1, p2, p3 = [box[k].astype(F32) for k in range(6)]
    ends = jnp.where(lane < PLANE, p2 * flags[1, 0], m2 * flags[-1, 0])
    padded = pltpu.roll(jnp.concatenate([field, ends], axis=1), 64, 1)
    first, inner, last = lane < 8, lane < 72, lane < 80
    above = jnp.where(
        first,
        pltpu.roll(m1, 72, 1) * flags[-1, 1],
        jnp.where(
            inner,
            pltpu.roll(p1, 8, 1) * flags[0, 1],
            jnp.where(last, pltpu.roll(p3, 72, 1) * flags[1, 1], 0.0),
        ),
    )
    below = jnp.where(
        first,
        pltpu.roll(m3, 8, 1) * flags[-1, -1],
        jnp.where(
            inner,
            pltpu.roll(m1, 72, 1) * flags[0, -1],
            jnp.where(last, pltpu.roll(p1, 8, 1) * flags[1, -1], 0.0),
        ),
    )
    halo = dot(jnp.concatenate([above, below], axis=1).astype(BF16), spread)
    return padded, halo


def windows(padded, halo, emit):
    lane = iota(padded.shape, 1)
    z = lane % 8
    y = (lane // 8) % 8
    for c in (-1, 0, 1):
        if c == 0:
            along = padded
        elif c == 1:
            along = jnp.where(z == 7, halo, pltpu.roll(padded, WIDE - 1, 1))
        else:
            along = jnp.where(z == 0, halo, pltpu.roll(padded, 1, 1))
        emit(3 + c + 1, along)
        emit(c + 1, jnp.where(y == 0, 0.0, pltpu.roll(along, 8, 1)))
        emit(6 + c + 1, jnp.where(y == 7, 0.0, pltpu.roll(along, WIDE - 8, 1)))


def kernel(
    nb,
    nr,
    total_bricks,
    mic_ref,
    tis_ref,
    nei_ref,
    w1_ref,
    b1_ref,
    w2_ref,
    b2_ref,
    hw_ref,
    hb_ref,
    cot_ref,
    pred_ref,
    fin_ref,
    s1_ref,
    s2_ref,
    w1p_ref,
    w2p_ref,
    front_ref,
    back_ref,
    a_ref,
    pick_ref,
    spread_ref,
    mic_out,
    h1_out,
    dz_out,
    mic_box,
    h1_box,
    dz_box,
    grad_ref,
    ra_ref,
    rb_src,
    rb_ref,
    w2_box,
    w2_sem,
    ex_send,
    ex_recv,
    a_send,
    a_recv,
    b_send,
    b_recv,
    gb_send,
    gb_recv,
    ga_send,
    ga_recv,
):
    me = lax.axis_index("brick")
    mr = lax.axis_index("region")
    channels = w2_ref.shape[0]
    rows = channels // nr

    fetch = pltpu.make_async_copy(w2_ref, w2_box, w2_sem)
    fetch.start()
    for box in (mic_box, h1_box, dz_box):
        box[...] = jnp.zeros_like(box)

    barrier = pltpu.get_barrier_semaphore()

    def greet_brick(step):
        pl.semaphore_signal(
            barrier, inc=1, device_id={"brick": (me + 1 + step) % nb}, device_id_type=MESH
        )

    for_each(nb - 1, greet_brick)
    for step in range(nr - 1):
        pl.semaphore_signal(
            barrier, inc=1, device_id={"region": (mr + 1 + step) % nr}, device_id_type=MESH
        )

    spot, slot = iota((CELLS, 128), 0), iota((CELLS, 128), 1)
    pick_ref[...] = jnp.where(
        spot == (slot % PLANE) * 8 + 7 * (slot // PLANE), 1.0, 0.0
    ).astype(BF16)
    pick = pick_ref[...]
    mic = jnp.broadcast_to(mic_ref[...].astype(F32), (MIC_ROWS, CELLS))
    pack(mic, pick, mic_out)

    def exchange(index, packet, box, act):
        for k, delta in enumerate(DELTAS):
            back = DELTAS.index(-delta)
            other = me + delta

            @pl.when((other >= 0) & (other < nb))
            def _():
                if act == "recv":
                    copy = pltpu.make_async_remote_copy(
                        src_ref=packet.at[1 if abs(delta) == 2 else 0],
                        dst_ref=box.at[k],
                        send_sem=ex_send.at[index, k],
                        recv_sem=ex_recv.at[index, k],
                        device_id={"brick": other},
                        device_id_type=MESH,
                    )
                    copy.wait_recv()
                else:
                    copy = pltpu.make_async_remote_copy(
                        src_ref=packet.at[1 if abs(delta) == 2 else 0],
                        dst_ref=box.at[back],
                        send_sem=ex_send.at[index, k],
                        recv_sem=ex_recv.at[index, back],
                        device_id={"brick": other},
                        device_id_type=MESH,
                    )
                    if act == "start":
                        copy.start()
                    else:
                        copy.wait_send()

    pl.semaphore_wait(barrier, nb - 1 + nr - 1)
    exchange(0, mic_out, mic_box, "start")

    spread_row, spread_lane = iota((256, WIDE), 0), iota((256, WIDE), 1)
    spread_ref[...] = jnp.where(
        spread_lane == (spread_row % 128) * 8 + 7 * (1 - spread_row // 128), 1.0, 0.0
    ).astype(BF16)
    w1p_ref[...] = jnp.zeros_like(w1p_ref)
    w1p_ref[:TAPS, :] = w1_ref[...]
    s1_ref[9 * channels :, :] = jnp.zeros((channels, WIDE), BF16)
    s2_ref[9 * channels :, :] = jnp.zeros((channels, WIDE), BF16)
    fetch.wait()
    w2p_ref[:, MAIN - 128 :] = jnp.zeros((channels, 128), BF16)
    w2p_ref[:, : TAPS * channels] = w2_box[...]
    taps_lane = iota((channels, WIDE), 1) < 9 * channels
    for a in range(3):
        view = w2p_ref[:, 512 * a + 64 * a - 64 * (a % 2) : 512 * a + 64 * a - 64 * (a % 2) + WIDE]
        if a % 2:
            view = pltpu.roll(view.astype(F32), WIDE - 64, 1)
        view = jnp.where(taps_lane, view.astype(F32), 0.0)
        front_ref[a * channels : (a + 1) * channels, :] = view.astype(BF16)
    flags = {}
    for a in (-1, 0, 1):
        for c in (-1, 0, 1):
            if (a, c) != (0, 0):
                flags[a, c] = jnp.where(nei_ref[0, direction_id(a, c)] >= 0, 1.0, 0.0).astype(F32)
    active = tis_ref[0, 0].astype(F32)
    bias1 = column(b1_ref[...])
    bias2 = column(b2_ref[...])
    bias3 = jnp.sum(
        jnp.where(iota((4, 4), 0) == iota((4, 4), 1), jnp.broadcast_to(hb_ref[...], (4, 4)), 0.0),
        axis=1,
        keepdims=True,
    )
    dpred = (cot_ref[...].astype(F32) * active / total_bricks).astype(BF16)
    dpred_wide = jnp.concatenate([dpred.astype(F32), jnp.zeros((4, CELLS), F32)], axis=0)
    d_second = lax.dot_general(
        hw_ref[...], dpred, (((0,), (0,)), ((), ())), preferred_element_type=F32
    )

    exchange(0, mic_out, mic_box, "recv")
    spread = spread_ref[...]
    padded, halo = widen(mic, mic_box, flags, spread)
    row = iota((MIC_ROWS, CELLS), 0)
    taps = [jnp.where((row >= 27) & (row < 30), 1.0, 0.0).astype(F32)]

    def emit_mic(index, value):
        rolled = pltpu.roll(value, WIDE - PLANE, 1)
        views = (value[:, :CELLS], rolled[:, :CELLS], value[:, 128:])
        for a in range(3):
            taps[0] = jnp.where(row == 9 * a + index, views[a], taps[0])

    windows(padded, halo, emit_mic)
    a_ref[...] = jnp.concatenate(
        [taps[0], dpred_wide, jnp.zeros((128 - MIC_ROWS - 8, CELLS), F32)], axis=0
    ).astype(BF16)
    z1 = (
        lax.dot_general(
            w1p_ref[...], a_ref[...], (((0,), (0,)), ((), ())), preferred_element_type=F32
        )
        + bias1
    )
    value1, slope1 = gelu_parts(z1)
    h1 = (value1 * active).astype(BF16).astype(F32)
    pack(h1, pick, h1_out)
    exchange(1, h1_out, h1_box, "start")
    slope1 = slope1 * active

    back = []
    for j in range(14):
        upper = w2p_ref[:, 128 * (13 - j) : 128 * (14 - j)].astype(F32)
        if j == 0:
            upper = jnp.where(iota((channels, 128), 1) < channels, upper, 0.0)
        if j < 13:
            lower = w2p_ref[:, 128 * (12 - j) : 128 * (13 - j)].astype(F32)
        else:
            lower = jnp.zeros((channels, 128), F32)
        turned = jnp.concatenate([upper, lower], axis=0).T
        back.append(
            jnp.where(iota((channels, 128), 1) < channels, turned[:channels], turned[channels:])
        )
    for a in range(3):
        first_tile = (9 * a) // 2
        view = jnp.concatenate(back[first_tile : first_tile + 5], axis=1)
        if a % 2:
            view = pltpu.roll(view, WIDE - 64, 1)
        view = jnp.where(taps_lane, view, 0.0)
        back_ref[a * channels : (a + 1) * channels, :] = view.astype(BF16)

    def store_windows(target):
        def emit(index, value):
            target[index * channels : (index + 1) * channels, :] = value.astype(BF16)

        return emit

    def convolve(weights, target):
        wide = dot(weights[...], target[...])
        middle = pltpu.roll(wide[channels : 2 * channels], WIDE - PLANE, 1)
        return (
            wide[:channels, :CELLS] + middle[:, :CELLS] + wide[2 * channels :, WIDE - CELLS :]
        )

    exchange(1, h1_out, h1_box, "recv")
    padded, halo = widen(h1, h1_box, flags, spread)
    windows(padded, halo, store_windows(s1_ref))
    z2 = convolve(front_ref, s1_ref) + bias2
    value2, slope2 = gelu_parts(z2)
    dz2 = (d_second * slope2 * active).astype(BF16)
    pack(dz2.astype(F32), pick, dz_out)
    exchange(2, dz_out, dz_box, "start")

    dz2_wide = dz2.astype(F32)
    gap = jnp.zeros((channels, 128), F32)
    left = jnp.concatenate([dz2_wide, gap], axis=1)
    stacked = jnp.concatenate(
        [left, pltpu.roll(left, PLANE, 1), jnp.concatenate([gap, dz2_wide], axis=1)], axis=0
    ).astype(BF16)
    grads = dot_nt(stacked, s1_ref[...])
    centre = pltpu.roll(grads[channels : 2 * channels], PLANE, 1)
    grad_ref[:, :512] = grads[:channels, :512].astype(BF16)
    grad_ref[:, 512:640] = (grads[:channels, 512:] + centre[:, :128]).astype(BF16)
    grad_ref[:, 640:1152] = centre[:, 128:].astype(BF16)
    grad_ref[:, 1152:MAIN] = grads[2 * channels :].astype(BF16)

    def region_copy(part, step, act):
        other = (mr + 1 + step) % nr
        lanes = pl.ds(0, MAIN) if part == 0 else pl.ds(MAIN, CHUNK)
        owner = other if act != "recv" else mr
        slot_id = mr if act != "recv" else other
        copy = pltpu.make_async_remote_copy(
            src_ref=grad_ref.at[pl.ds(pl.multiple_of(owner * rows, rows), rows), lanes],
            dst_ref=ra_ref.at[slot_id, :, lanes],
            send_sem=a_send.at[part, other],
            recv_sem=a_recv.at[part, slot_id],
            device_id={"region": other},
            device_id_type=MESH,
        )
        if act == "start":
            copy.start()
        elif act == "recv":
            copy.wait_recv()
        else:
            copy.wait_send()

    for step in range(nr - 1):
        region_copy(0, step, "start")

    h2 = (value2 * active).astype(BF16)
    linear = dot(hw_ref[...], h2) + bias3
    pred_ref[...] = (linear * active).astype(BF16)
    tap_rows = a_ref[...]
    dpred_tall = jnp.concatenate(
        [dpred_wide, jnp.zeros((channels - 8, CELLS), F32)], axis=0
    ).astype(BF16)
    lane = iota((channels, 128), 1)
    small = jnp.where(lane == 28, dot_nt(dz2, tap_rows), 0.0)
    small = small + jnp.where((lane >= 32) & (lane < 36), dot_nt(h2, tap_rows), 0.0)
    small = small + jnp.where(lane == 29, dot_nt(dpred_tall, tap_rows), 0.0)

    def brick_copy(chunk, act):
        @pl.when(me != chunk)
        def _():
            copy = pltpu.make_async_remote_copy(
                src_ref=rb_src.at[chunk],
                dst_ref=rb_ref.at[me],
                send_sem=b_send.at[chunk],
                recv_sem=b_recv.at[me],
                device_id={"brick": chunk},
                device_id_type=MESH,
            )
            if act == "start":
                copy.start()
            else:
                copy.wait_send()

    mine = pl.ds(pl.multiple_of(mr * rows, rows), rows)

    def region_sum(part):
        lanes = pl.ds(0, MAIN) if part == 0 else pl.ds(MAIN, CHUNK)
        for step in range(nr - 1):
            region_copy(part, step, "recv")
        total = grad_ref[mine, lanes].astype(F32)
        for step in range(nr - 1):
            total = total + ra_ref[(mr + 1 + step) % nr, :, lanes].astype(F32)
        return total

    exchange(2, dz_out, dz_box, "recv")
    padded, halo = widen(dz2.astype(F32), dz_box, flags, spread)
    windows(padded, halo, store_windows(s2_ref))
    total = region_sum(0)
    for chunk in range(CHUNKS - 1):
        rb_src[chunk] = total[:, CHUNK * chunk : CHUNK * (chunk + 1)].astype(BF16)
        brick_copy(chunk, "start")
    dz1 = (convolve(back_ref, s2_ref) * slope1).astype(BF16)
    small = small + jnp.where(lane < 28, dot_nt(dz1, tap_rows), 0.0)
    grad_ref[:, MAIN:] = halves(small)
    for step in range(nr - 1):
        region_copy(1, step, "start")

    def gather_copy(step, act):
        other = (me + 1 + step) % nb
        copy = pltpu.make_async_remote_copy(
            src_ref=fin_ref.at[mr, me % CHUNKS],
            dst_ref=fin_ref.at[mr, me % CHUNKS],
            send_sem=gb_send.at[other],
            recv_sem=gb_recv.at[me % CHUNKS],
            device_id={"brick": other},
            device_id_type=MESH,
        )
        if act == "start":
            copy.start()
        else:
            copy.wait_send()

    def own(final):
        def arrived(step):
            other = (me + 1 + step) % nb
            pltpu.make_async_remote_copy(
                src_ref=rb_src.at[0],
                dst_ref=rb_ref.at[other],
                send_sem=b_send.at[0],
                recv_sem=b_recv.at[other],
                device_id={"brick": other},
                device_id_type=MESH,
            ).wait_recv()

        for_each(nb - 1, arrived)
        kept = rb_src[me % CHUNKS].astype(F32)
        if nb <= CHUNKS:
            for step in range(nb - 1):
                kept = kept + rb_ref[(me + 1 + step) % nb].astype(F32)
        else:
            kept = lax.fori_loop(
                0, nb - 1, lambda step, s: s + rb_ref[(me + 1 + step) % nb].astype(F32), kept
            )
        fin_ref[mr, me % CHUNKS] = halves(joined(kept)) if final else kept.astype(BF16)
        for_each(nb - 1, lambda step: gather_copy(step, "start"))

    def spread_copy(chunk, step, act):
        other = (mr + 1 + step) % nr
        slot_id = other if act == "recv" else mr
        copy = pltpu.make_async_remote_copy(
            src_ref=fin_ref.at[slot_id, chunk],
            dst_ref=fin_ref.at[slot_id, chunk],
            send_sem=ga_send.at[other, chunk],
            recv_sem=ga_recv.at[slot_id, chunk],
            device_id={"region": other},
            device_id_type=MESH,
        )
        if act == "start":
            copy.start()
        elif act == "recv":
            copy.wait_recv()
        else:
            copy.wait_send()

    pl.when(me < CHUNKS - 1)(lambda: own(False))
    rb_src[CHUNKS - 1] = halves(joined(region_sum(1)))
    brick_copy(CHUNKS - 1, "start")
    pl.when(me == CHUNKS - 1)(lambda: own(True))

    for chunk in range(CHUNKS):
        @pl.when(me != chunk)
        def _():
            pltpu.make_async_remote_copy(
                src_ref=fin_ref.at[mr, chunk],
                dst_ref=fin_ref.at[mr, chunk],
                send_sem=gb_send.at[chunk],
                recv_sem=gb_recv.at[chunk],
                device_id={"brick": chunk},
                device_id_type=MESH,
            ).wait_recv()

        for step in range(nr - 1):
            spread_copy(chunk, step, "start")

    exchange(0, mic_out, mic_box, "sent")
    exchange(1, h1_out, h1_box, "sent")
    exchange(2, dz_out, dz_box, "sent")
    for part in range(2):
        for step in range(nr - 1):
            region_copy(part, step, "sent")
    for chunk in range(CHUNKS):
        brick_copy(chunk, "sent")
    if nb > CHUNKS:
        pl.when(me < CHUNKS)(lambda: for_each(nb - 1, lambda step: gather_copy(step, "sent")))
    else:
        for_each(nb - 1, lambda step: gather_copy(step, "sent"))
    for chunk in range(CHUNKS):
        for step in range(nr - 1):
            spread_copy(chunk, step, "recv")
            spread_copy(chunk, step, "sent")


def finish(
    fin_ref, raw_ref, pred_ref, gw1_ref, gb1_ref, gw2_ref, gb2_ref, gwh_ref, gbh_ref
):
    nr, _, rows, _ = fin_ref.shape
    channels = nr * rows
    pred_ref[...] = raw_ref[...]
    for region in range(nr):
        where = slice(region * rows, (region + 1) * rows)
        for chunk in range(CHUNKS - 1):
            block = fin_ref[region, chunk].astype(F32)
            if chunk < CHUNKS - 2:
                gw2_ref[where, CHUNK * chunk : CHUNK * (chunk + 1)] = block
            else:
                gw2_ref[where, CHUNK * chunk : CHUNK * chunk + 128] = block[:, :128]
                gw2_ref[where, CHUNK * chunk + 128 : TAPS * channels] = block[
                    :, 128 : TAPS * channels - CHUNK * chunk
                ]
    small = jnp.concatenate(
        [joined(fin_ref[region, CHUNKS - 1]) for region in range(nr)], axis=0
    )
    turned = jnp.concatenate([small, jnp.zeros((128 - channels, 128), F32)], axis=0).T
    gw1_ref[...] = turned[:TAPS, :channels]
    gb1_ref[...] = turned[27:28, :channels]
    gb2_ref[...] = turned[28:29, :channels]
    gbh_ref[...] = turned[29:30, :4]
    gwh_ref[...] = turned[32:36, :channels]


def solution(mesh):
    nb, nr = mesh.shape["brick"], mesh.shape["region"]

    def shards(mic, tissue, neighbours, w1, b1, w2, b2, hw, hb, cot):
        channels = w1.shape[0]
        rows = channels // nr
        vmem = pl.BlockSpec(memory_space=pltpu.VMEM)
        smem = pl.BlockSpec(memory_space=pltpu.SMEM)
        dma = pltpu.SemaphoreType.DMA
        total_bricks = nb * nr * mic.shape[1]
        outs = pl.pallas_call(
            functools.partial(kernel, nb, nr, total_bricks),
            out_shape=(
                jax.ShapeDtypeStruct((4, CELLS), BF16),
                jax.ShapeDtypeStruct((nr, CHUNKS, rows, CHUNK), BF16),
            ),
            in_specs=[vmem, smem, smem, vmem, vmem, pl.BlockSpec(memory_space=pl.ANY)] + [vmem] * 4,
            out_specs=(vmem,) * 2,
            scratch_shapes=[
                pltpu.VMEM((WIDE, WIDE), BF16),
                pltpu.VMEM((WIDE, WIDE), BF16),
                pltpu.VMEM((128, channels), BF16),
                pltpu.VMEM((channels, MAIN), BF16),
                pltpu.VMEM((3 * channels, WIDE), BF16),
                pltpu.VMEM((3 * channels, WIDE), BF16),
                pltpu.VMEM((128, CELLS), BF16),
                pltpu.VMEM((CELLS, 128), BF16),
                pltpu.VMEM((256, WIDE), BF16),
                pltpu.VMEM((2, MIC_ROWS, 128), BF16),
                pltpu.VMEM((2, channels, 128), BF16),
                pltpu.VMEM((2, channels, 128), BF16),
                pltpu.VMEM((6, MIC_ROWS, 128), BF16),
                pltpu.VMEM((6, channels, 128), BF16),
                pltpu.VMEM((6, channels, 128), BF16),
                pltpu.VMEM((channels, MAIN + CHUNK), BF16),
                pltpu.VMEM((nr, rows, MAIN + CHUNK), BF16),
                pltpu.VMEM((CHUNKS, rows, CHUNK), BF16),
                pltpu.VMEM((nb, rows, CHUNK), BF16),
                pltpu.VMEM((channels, TAPS * channels), BF16),
                dma,
                dma((3, 6)),
                dma((3, 6)),
                dma((2, nr)),
                dma((2, nr)),
                dma((CHUNKS,)),
                dma((nb,)),
                dma((nb,)),
                dma((CHUNKS,)),
                dma((nr, CHUNKS)),
                dma((nr, CHUNKS)),
            ],
            compiler_params=pltpu.CompilerParams(
                collective_id=0, has_side_effects=True, vmem_limit_bytes=40 * 1024 * 1024
            ),
            cost_estimate=pl.CostEstimate(flops=360_000_000, bytes_accessed=2_000_000, transcendentals=65536),
        )(
            mic.reshape(1, CELLS),
            tissue,
            neighbours.reshape(1, 26),
            w1.T,
            b1.reshape(1, channels),
            w2,
            b2.reshape(1, channels),
            hw,
            hb.reshape(1, 4),
            cot.reshape(4, CELLS),
        )
        pred, gw1, gb1, gw2, gb2, gwh, gbh = pl.pallas_call(
            finish,
            out_shape=(
                jax.ShapeDtypeStruct((4, CELLS), BF16),
                jax.ShapeDtypeStruct((TAPS, channels), F32),
                jax.ShapeDtypeStruct((1, channels), F32),
                jax.ShapeDtypeStruct((channels, TAPS * channels), F32),
                jax.ShapeDtypeStruct((1, channels), F32),
                jax.ShapeDtypeStruct((4, channels), F32),
                jax.ShapeDtypeStruct((1, 4), F32),
            ),
            in_specs=[vmem] * 2,
            out_specs=(vmem,) * 7,
        )(outs[1], outs[0])
        return (
            pred.reshape(1, 1, 4, CELLS),
            gw1.T,
            gb1.reshape(channels),
            gw2,
            gb2.reshape(channels),
            gwh,
            gbh.reshape(4),
        )

    return jax.shard_map(
        shards,
        mesh=mesh,
        in_specs=(
            P("region", "brick", None),
            P("region", "brick"),
            P("region", "brick", None),
            P(),
            P(),
            P(),
            P(),
            P(),
            P(),
            P("region", "brick", None, None),
        ),
        out_specs=(P("region", "brick", None, None), P(), P(), P(), P(), P(), P()),
        check_vma=False,
    )
```

```python
import functools
import math

import jax
import jax.numpy as jnp
from jax import lax
from jax.experimental import pallas as pl
from jax.experimental.pallas import tpu as pltpu
from jax.sharding import PartitionSpec as P

F32 = jnp.float32
BF16 = jnp.bfloat16
MESH = pl.DeviceIdType.MESH
TAPS = 27
PLANE = 64
CELLS = 512
WIDE = 640
DELTAS = (-3, -2, -1, 1, 2, 3)
CHUNKS = 8
CHUNK = 256
MAIN = 7 * CHUNK
MIC_ROWS = 32
SLOPE = math.sqrt(2 / math.pi)
CUBIC = 0.044715


def direction_id(a, c):
    full = (a + 1) * 9 + 3 + (c + 1)
    return full if full < 13 else full - 1


def iota(shape, dim):
    return lax.broadcasted_iota(jnp.int32, shape, dim)


def dot(left, right):
    return lax.dot_general(left, right, (((1,), (0,)), ((), ())), preferred_element_type=F32)


def dot_nt(left, right):
    return lax.dot_general(left, right, (((1,), (1,)), ((), ())), preferred_element_type=F32)


def column(row):
    size = row.shape[1]
    wide = jnp.broadcast_to(row, (size, size))
    return jnp.sum(jnp.where(iota((size, size), 0) == iota((size, size), 1), wide, 0.0), axis=1, keepdims=True)


def gelu_parts(values):
    square = values * values
    bent = jnp.tanh(SLOPE * (values + CUBIC * square * values))
    half = 0.5 * (1.0 + bent)
    slope = half + 0.5 * values * (1.0 - bent * bent) * (SLOPE * (1.0 + 3.0 * CUBIC * square))
    return values * half, slope


def halves(values):
    high = values.astype(BF16)
    return jnp.concatenate([high, (values - high.astype(F32)).astype(BF16)], axis=1)


def joined(pair):
    return pair[:, :128].astype(F32) + pair[:, 128:].astype(F32)


def for_each(count, body):
    if count <= 8:
        for step in range(count):
            body(step)
    else:
        def step_body(step, carry):
            body(step)
            return carry

        lax.fori_loop(0, count, step_body, 0)


def pack(field, pick, packet):
    rows = field.shape[0]
    low = iota((rows, 128), 1) < PLANE
    packet[0] = dot(field.astype(BF16), pick).astype(BF16)
    packet[1] = jnp.where(low, field[:, :128], field[:, CELLS - 128 :]).astype(BF16)


def widen(field, box, flags, spread):
    rows = field.shape[0]
    lane = iota((rows, 128), 1)
    m3, m2, m1, p1, p2, p3 = [box[k].astype(F32) for k in range(6)]
    ends = jnp.where(lane < PLANE, p2 * flags[1, 0], m2 * flags[-1, 0])
    padded = pltpu.roll(jnp.concatenate([field, ends], axis=1), 64, 1)
    first, inner, last = lane < 8, lane < 72, lane < 80
    above = jnp.where(
        first,
        pltpu.roll(m1, 72, 1) * flags[-1, 1],
        jnp.where(
            inner,
            pltpu.roll(p1, 8, 1) * flags[0, 1],
            jnp.where(last, pltpu.roll(p3, 72, 1) * flags[1, 1], 0.0),
        ),
    )
    below = jnp.where(
        first,
        pltpu.roll(m3, 8, 1) * flags[-1, -1],
        jnp.where(
            inner,
            pltpu.roll(m1, 72, 1) * flags[0, -1],
            jnp.where(last, pltpu.roll(p1, 8, 1) * flags[1, -1], 0.0),
        ),
    )
    halo = dot(jnp.concatenate([above, below], axis=1).astype(BF16), spread)
    return padded, halo


def windows(padded, halo, emit):
    row = iota((1, WIDE), 1)
    z = jnp.broadcast_to(row & 7, padded.shape)
    y = jnp.broadcast_to(row & 56, padded.shape)
    for c in (-1, 0, 1):
        if c == 0:
            along = padded
        elif c == 1:
            along = jnp.where(z == 7, halo, pltpu.roll(padded, WIDE - 1, 1))
        else:
            along = jnp.where(z == 0, halo, pltpu.roll(padded, 1, 1))
        emit(3 + c + 1, along)
        emit(c + 1, jnp.where(y == 0, 0.0, pltpu.roll(along, 8, 1)))
        emit(6 + c + 1, jnp.where(y == 56, 0.0, pltpu.roll(along, WIDE - 8, 1)))


def kernel(
    nb,
    nr,
    total_bricks,
    mic_hbm,
    tis_ref,
    nei_ref,
    w1_hbm,
    b1_hbm,
    w2_hbm,
    b2_hbm,
    hw_hbm,
    hb_hbm,
    cot_hbm,
    pred_ref,
    fin_ref,
    s1_ref,
    s2_ref,
    w1p_ref,
    w2p_ref,
    front_ref,
    back_ref,
    a_ref,
    pick_ref,
    spread_ref,
    mic_out,
    h1_out,
    dz_out,
    mic_box,
    h1_box,
    dz_box,
    grad_ref,
    ra_ref,
    rb_src,
    rb_ref,
    mic_ref,
    w1_ref,
    b1_ref,
    w2_ref,
    b2_ref,
    hw_ref,
    hb_ref,
    cot_ref,
    in_sem,
    ex_send,
    ex_recv,
    a_send,
    a_recv,
    b_send,
    b_recv,
    gb_send,
    gb_recv,
    ga_send,
    ga_recv,
):
    me = lax.axis_index("brick")
    mr = lax.axis_index("region")
    channels = w2_ref.shape[0]
    rows = channels // nr

    sources = (mic_hbm, w1_hbm, b1_hbm, w2_hbm, b2_hbm, hw_hbm, hb_hbm, cot_hbm)
    places = (mic_ref, w1_ref, b1_ref, w2_ref, b2_ref, hw_ref, hb_ref, cot_ref)
    fetches = [
        pltpu.make_async_copy(source, place, in_sem.at[k])
        for k, (source, place) in enumerate(zip(sources, places))
    ]
    fetches[0].start()
    for box in (mic_box, h1_box, dz_box):
        box[...] = jnp.zeros_like(box)

    barrier = pltpu.get_barrier_semaphore()

    def greet_brick(step):
        pl.semaphore_signal(
            barrier, inc=1, device_id={"brick": (me + 1 + step) % nb}, device_id_type=MESH
        )

    for_each(nb - 1, greet_brick)
    for step in range(nr - 1):
        pl.semaphore_signal(
            barrier, inc=1, device_id={"region": (mr + 1 + step) % nr}, device_id_type=MESH
        )

    for fetch in fetches[1:]:
        fetch.start()

    spot, slot = iota((CELLS, 128), 0), iota((CELLS, 128), 1)
    pick_ref[...] = jnp.where(
        spot == (slot & 63) * 8 + 7 * (slot >> 6), 1.0, 0.0
    ).astype(BF16)
    pick = pick_ref[...]
    fetches[0].wait()
    mic = jnp.broadcast_to(mic_ref[...].astype(F32), (MIC_ROWS, CELLS))
    pack(mic, pick, mic_out)

    def exchange(index, packet, box, act):
        for k, delta in enumerate(DELTAS):
            back = DELTAS.index(-delta)
            other = me + delta

            @pl.when((other >= 0) & (other < nb))
            def _():
                if act == "recv":
                    copy = pltpu.make_async_remote_copy(
                        src_ref=packet.at[1 if abs(delta) == 2 else 0],
                        dst_ref=box.at[k],
                        send_sem=ex_send.at[index, k],
                        recv_sem=ex_recv.at[index, k],
                        device_id={"brick": other},
                        device_id_type=MESH,
                    )
                    copy.wait_recv()
                else:
                    copy = pltpu.make_async_remote_copy(
                        src_ref=packet.at[1 if abs(delta) == 2 else 0],
                        dst_ref=box.at[back],
                        send_sem=ex_send.at[index, k],
                        recv_sem=ex_recv.at[index, back],
                        device_id={"brick": other},
                        device_id_type=MESH,
                    )
                    if act == "start":
                        copy.start()
                    else:
                        copy.wait_send()

    pl.semaphore_wait(barrier, nb - 1 + nr - 1)
    exchange(0, mic_out, mic_box, "start")

    spread_row, spread_lane = iota((256, WIDE), 0), iota((256, WIDE), 1)
    spread_ref[...] = jnp.where(
        spread_lane == (spread_row & 127) * 8 + 7 - 7 * (spread_row >> 7), 1.0, 0.0
    ).astype(BF16)
    for fetch in fetches[1:]:
        fetch.wait()
    w1p_ref[...] = jnp.zeros_like(w1p_ref)
    w1p_ref[:TAPS, :] = w1_ref[...]
    s1_ref[9 * channels :, :] = jnp.zeros((channels, WIDE), BF16)
    s2_ref[9 * channels :, :] = jnp.zeros((channels, WIDE), BF16)
    w2p_ref[:, MAIN - 128 :] = jnp.zeros((channels, 128), BF16)
    w2p_ref[:, : TAPS * channels] = w2_ref[...]
    taps_lane = iota((channels, WIDE), 1) < 9 * channels
    for a in range(3):
        view = w2p_ref[:, 512 * a + 64 * a - 64 * (a % 2) : 512 * a + 64 * a - 64 * (a % 2) + WIDE]
        if a % 2:
            view = pltpu.roll(view.astype(F32), WIDE - 64, 1)
        view = jnp.where(taps_lane, view.astype(F32), 0.0)
        front_ref[a * channels : (a + 1) * channels, :] = view.astype(BF16)
    flags = {}
    for a in (-1, 0, 1):
        for c in (-1, 0, 1):
            if (a, c) != (0, 0):
                flags[a, c] = jnp.where(nei_ref[0, direction_id(a, c)] >= 0, 1.0, 0.0).astype(F32)
    active = tis_ref[0, 0].astype(F32)
    bias1 = column(b1_ref[...])
    bias2 = column(b2_ref[...])
    bias3 = jnp.sum(
        jnp.where(iota((4, 4), 0) == iota((4, 4), 1), jnp.broadcast_to(hb_ref[...], (4, 4)), 0.0),
        axis=1,
        keepdims=True,
    )
    dpred = (cot_ref[...].astype(F32) * active / total_bricks).astype(BF16)
    dpred_wide = jnp.concatenate([dpred.astype(F32), jnp.zeros((4, CELLS), F32)], axis=0)
    d_second = lax.dot_general(
        hw_ref[...], dpred, (((0,), (0,)), ((), ())), preferred_element_type=F32
    )

    exchange(0, mic_out, mic_box, "recv")
    spread = spread_ref[...]
    padded, halo = widen(mic, mic_box, flags, spread)
    row = iota((MIC_ROWS, CELLS), 0)
    taps = [jnp.where((row >= 27) & (row < 30), 1.0, 0.0).astype(F32)]

    def emit_mic(index, value):
        rolled = pltpu.roll(value, WIDE - PLANE, 1)
        views = (value[:, :CELLS], rolled[:, :CELLS], value[:, 128:])
        for a in range(3):
            taps[0] = jnp.where(row == 9 * a + index, views[a], taps[0])

    windows(padded, halo, emit_mic)
    a_ref[...] = jnp.concatenate(
        [taps[0], dpred_wide, jnp.zeros((128 - MIC_ROWS - 8, CELLS), F32)], axis=0
    ).astype(BF16)
    z1 = (
        lax.dot_general(
            w1p_ref[...], a_ref[...], (((0,), (0,)), ((), ())), preferred_element_type=F32
        )
        + bias1
    )
    value1, slope1 = gelu_parts(z1)
    h1 = (value1 * active).astype(BF16).astype(F32)
    pack(h1, pick, h1_out)
    exchange(1, h1_out, h1_box, "start")
    slope1 = slope1 * active

    back = []
    for j in range(14):
        upper = w2p_ref[:, 128 * (13 - j) : 128 * (14 - j)].astype(F32)
        if j == 0:
            upper = jnp.where(iota((channels, 128), 1) < channels, upper, 0.0)
        if j < 13:
            lower = w2p_ref[:, 128 * (12 - j) : 128 * (13 - j)].astype(F32)
        else:
            lower = jnp.zeros((channels, 128), F32)
        turned = jnp.concatenate([upper, lower], axis=0).T
        back.append(
            jnp.where(iota((channels, 128), 1) < channels, turned[:channels], turned[channels:])
        )
    for a in range(3):
        first_tile = (9 * a) // 2
        view = jnp.concatenate(back[first_tile : first_tile + 5], axis=1)
        if a % 2:
            view = pltpu.roll(view, WIDE - 64, 1)
        view = jnp.where(taps_lane, view, 0.0)
        back_ref[a * channels : (a + 1) * channels, :] = view.astype(BF16)

    def store_windows(target):
        def emit(index, value):
            target[index * channels : (index + 1) * channels, :] = value.astype(BF16)

        return emit

    def convolve(weights, target):
        wide = dot(weights[...], target[...])
        middle = pltpu.roll(wide[channels : 2 * channels], WIDE - PLANE, 1)
        return (
            wide[:channels, :CELLS] + middle[:, :CELLS] + wide[2 * channels :, WIDE - CELLS :]
        )

    exchange(1, h1_out, h1_box, "recv")
    padded, halo = widen(h1, h1_box, flags, spread)
    windows(padded, halo, store_windows(s1_ref))
    z2 = convolve(front_ref, s1_ref) + bias2
    value2, slope2 = gelu_parts(z2)
    dz2 = (d_second * slope2 * active).astype(BF16)
    pack(dz2.astype(F32), pick, dz_out)
    exchange(2, dz_out, dz_box, "start")

    dz2_wide = dz2.astype(F32)
    gap = jnp.zeros((channels, 128), F32)
    left = jnp.concatenate([dz2_wide, gap], axis=1)
    stacked = jnp.concatenate(
        [left, pltpu.roll(left, PLANE, 1), jnp.concatenate([gap, dz2_wide], axis=1)], axis=0
    ).astype(BF16)
    grads = dot_nt(stacked, s1_ref[...])
    centre = pltpu.roll(grads[channels : 2 * channels], PLANE, 1)
    grad_ref[:, :512] = grads[:channels, :512].astype(BF16)
    grad_ref[:, 512:640] = (grads[:channels, 512:] + centre[:, :128]).astype(BF16)
    grad_ref[:, 640:1152] = centre[:, 128:].astype(BF16)
    grad_ref[:, 1152:MAIN] = grads[2 * channels :].astype(BF16)

    def region_copy(part, step, act):
        other = (mr + 1 + step) % nr
        lanes = pl.ds(0, MAIN) if part == 0 else pl.ds(MAIN, CHUNK)
        owner = other if act != "recv" else mr
        slot_id = mr if act != "recv" else other
        copy = pltpu.make_async_remote_copy(
            src_ref=grad_ref.at[pl.ds(pl.multiple_of(owner * rows, rows), rows), lanes],
            dst_ref=ra_ref.at[slot_id, :, lanes],
            send_sem=a_send.at[part, other],
            recv_sem=a_recv.at[part, slot_id],
            device_id={"region": other},
            device_id_type=MESH,
        )
        if act == "start":
            copy.start()
        elif act == "recv":
            copy.wait_recv()
        else:
            copy.wait_send()

    for step in range(nr - 1):
        region_copy(0, step, "start")

    h2 = (value2 * active).astype(BF16)
    linear = dot(hw_ref[...], h2) + bias3
    pred_ref[...] = (linear * active).astype(BF16)
    tap_rows = a_ref[...]
    dpred_tall = jnp.concatenate(
        [dpred_wide, jnp.zeros((channels - 8, CELLS), F32)], axis=0
    ).astype(BF16)
    lane = iota((channels, 128), 1)
    small = jnp.where(lane == 28, dot_nt(dz2, tap_rows), 0.0)
    small = small + jnp.where((lane >= 32) & (lane < 36), dot_nt(h2, tap_rows), 0.0)
    small = small + jnp.where(lane == 29, dot_nt(dpred_tall, tap_rows), 0.0)

    def brick_copy(chunk, act):
        @pl.when(me != chunk)
        def _():
            copy = pltpu.make_async_remote_copy(
                src_ref=rb_src.at[chunk],
                dst_ref=rb_ref.at[me],
                send_sem=b_send.at[chunk],
                recv_sem=b_recv.at[me],
                device_id={"brick": chunk},
                device_id_type=MESH,
            )
            if act == "start":
                copy.start()
            else:
                copy.wait_send()

    mine = pl.ds(pl.multiple_of(mr * rows, rows), rows)

    def region_sum(part):
        lanes = pl.ds(0, MAIN) if part == 0 else pl.ds(MAIN, CHUNK)
        for step in range(nr - 1):
            region_copy(part, step, "recv")
        total = grad_ref[mine, lanes].astype(F32)
        for step in range(nr - 1):
            total = total + ra_ref[(mr + 1 + step) % nr, :, lanes].astype(F32)
        return total

    exchange(2, dz_out, dz_box, "recv")
    padded, halo = widen(dz2.astype(F32), dz_box, flags, spread)
    windows(padded, halo, store_windows(s2_ref))
    total = region_sum(0)
    for chunk in range(CHUNKS - 1):
        rb_src[chunk] = total[:, CHUNK * chunk : CHUNK * (chunk + 1)].astype(BF16)
        brick_copy(chunk, "start")
    dz1 = (convolve(back_ref, s2_ref) * slope1).astype(BF16)
    small = small + jnp.where(lane < 28, dot_nt(dz1, tap_rows), 0.0)
    grad_ref[:, MAIN:] = halves(small)
    for step in range(nr - 1):
        region_copy(1, step, "start")

    def gather_copy(step, act):
        other = (me + 1 + step) % nb
        copy = pltpu.make_async_remote_copy(
            src_ref=fin_ref.at[mr, me % CHUNKS],
            dst_ref=fin_ref.at[mr, me % CHUNKS],
            send_sem=gb_send.at[other],
            recv_sem=gb_recv.at[me % CHUNKS],
            device_id={"brick": other},
            device_id_type=MESH,
        )
        if act == "start":
            copy.start()
        else:
            copy.wait_send()

    def own(final):
        def arrived(step):
            other = (me + 1 + step) % nb
            pltpu.make_async_remote_copy(
                src_ref=rb_src.at[0],
                dst_ref=rb_ref.at[other],
                send_sem=b_send.at[0],
                recv_sem=b_recv.at[other],
                device_id={"brick": other},
                device_id_type=MESH,
            ).wait_recv()

        for_each(nb - 1, arrived)
        kept = rb_src[me % CHUNKS].astype(F32)
        if nb <= CHUNKS:
            for step in range(nb - 1):
                kept = kept + rb_ref[(me + 1 + step) % nb].astype(F32)
        else:
            kept = lax.fori_loop(
                0, nb - 1, lambda step, s: s + rb_ref[(me + 1 + step) % nb].astype(F32), kept
            )
        fin_ref[mr, me % CHUNKS] = halves(joined(kept)) if final else kept.astype(BF16)
        for_each(nb - 1, lambda step: gather_copy(step, "start"))

    def spread_copy(chunk, step, act):
        other = (mr + 1 + step) % nr
        slot_id = other if act == "recv" else mr
        copy = pltpu.make_async_remote_copy(
            src_ref=fin_ref.at[slot_id, chunk],
            dst_ref=fin_ref.at[slot_id, chunk],
            send_sem=ga_send.at[other, chunk],
            recv_sem=ga_recv.at[slot_id, chunk],
            device_id={"region": other},
            device_id_type=MESH,
        )
        if act == "start":
            copy.start()
        elif act == "recv":
            copy.wait_recv()
        else:
            copy.wait_send()

    pl.when(me < CHUNKS - 1)(lambda: own(False))
    rb_src[CHUNKS - 1] = halves(joined(region_sum(1)))
    brick_copy(CHUNKS - 1, "start")
    pl.when(me == CHUNKS - 1)(lambda: own(True))

    for chunk in range(CHUNKS):
        @pl.when(me != chunk)
        def _():
            pltpu.make_async_remote_copy(
                src_ref=fin_ref.at[mr, chunk],
                dst_ref=fin_ref.at[mr, chunk],
                send_sem=gb_send.at[chunk],
                recv_sem=gb_recv.at[chunk],
                device_id={"brick": chunk},
                device_id_type=MESH,
            ).wait_recv()

        for step in range(nr - 1):
            spread_copy(chunk, step, "start")

    exchange(0, mic_out, mic_box, "sent")
    exchange(1, h1_out, h1_box, "sent")
    exchange(2, dz_out, dz_box, "sent")
    for part in range(2):
        for step in range(nr - 1):
            region_copy(part, step, "sent")
    for chunk in range(CHUNKS):
        brick_copy(chunk, "sent")
    if nb > CHUNKS:
        pl.when(me < CHUNKS)(lambda: for_each(nb - 1, lambda step: gather_copy(step, "sent")))
    else:
        for_each(nb - 1, lambda step: gather_copy(step, "sent"))
    for chunk in range(CHUNKS):
        for step in range(nr - 1):
            spread_copy(chunk, step, "recv")
            spread_copy(chunk, step, "sent")


def finish(
    fin_ref, raw_ref, pred_ref, gw1_ref, gb1_ref, gw2_ref, gb2_ref, gwh_ref, gbh_ref
):
    nr, _, rows, _ = fin_ref.shape
    channels = nr * rows
    pred_ref[...] = raw_ref[...]
    for region in range(nr):
        where = slice(region * rows, (region + 1) * rows)
        for chunk in range(CHUNKS - 1):
            block = fin_ref[region, chunk].astype(F32)
            if chunk < CHUNKS - 2:
                gw2_ref[where, CHUNK * chunk : CHUNK * (chunk + 1)] = block
            else:
                gw2_ref[where, CHUNK * chunk : CHUNK * chunk + 128] = block[:, :128]
                gw2_ref[where, CHUNK * chunk + 128 : TAPS * channels] = block[
                    :, 128 : TAPS * channels - CHUNK * chunk
                ]
    small = jnp.concatenate(
        [joined(fin_ref[region, CHUNKS - 1]) for region in range(nr)], axis=0
    )
    turned = jnp.concatenate([small, jnp.zeros((128 - channels, 128), F32)], axis=0).T
    gw1_ref[...] = turned[:TAPS, :channels]
    gb1_ref[...] = turned[27:28, :channels]
    gb2_ref[...] = turned[28:29, :channels]
    gbh_ref[...] = turned[29:30, :4]
    gwh_ref[...] = turned[32:36, :channels]


def solution(mesh):
    nb, nr = mesh.shape["brick"], mesh.shape["region"]

    def shards(mic, tissue, neighbours, w1, b1, w2, b2, hw, hb, cot):
        channels = w1.shape[0]
        rows = channels // nr
        vmem = pl.BlockSpec(memory_space=pltpu.VMEM)
        hbm = pl.BlockSpec(memory_space=pl.ANY)
        smem = pl.BlockSpec(memory_space=pltpu.SMEM)
        dma = pltpu.SemaphoreType.DMA
        total_bricks = nb * nr * mic.shape[1]
        outs = pl.pallas_call(
            functools.partial(kernel, nb, nr, total_bricks),
            out_shape=(
                jax.ShapeDtypeStruct((4, CELLS), BF16),
                jax.ShapeDtypeStruct((nr, CHUNKS, rows, CHUNK), BF16),
            ),
            in_specs=[hbm, smem, smem] + [hbm] * 7,
            out_specs=(vmem,) * 2,
            scratch_shapes=[
                pltpu.VMEM((WIDE, WIDE), BF16),
                pltpu.VMEM((WIDE, WIDE), BF16),
                pltpu.VMEM((128, channels), BF16),
                pltpu.VMEM((channels, MAIN), BF16),
                pltpu.VMEM((3 * channels, WIDE), BF16),
                pltpu.VMEM((3 * channels, WIDE), BF16),
                pltpu.VMEM((128, CELLS), BF16),
                pltpu.VMEM((CELLS, 128), BF16),
                pltpu.VMEM((256, WIDE), BF16),
                pltpu.VMEM((2, MIC_ROWS, 128), BF16),
                pltpu.VMEM((2, channels, 128), BF16),
                pltpu.VMEM((2, channels, 128), BF16),
                pltpu.VMEM((6, MIC_ROWS, 128), BF16),
                pltpu.VMEM((6, channels, 128), BF16),
                pltpu.VMEM((6, channels, 128), BF16),
                pltpu.VMEM((channels, MAIN + CHUNK), BF16),
                pltpu.VMEM((nr, rows, MAIN + CHUNK), BF16),
                pltpu.VMEM((CHUNKS, rows, CHUNK), BF16),
                pltpu.VMEM((nb, rows, CHUNK), BF16),
                pltpu.VMEM((1, CELLS), BF16),
                pltpu.VMEM((TAPS, channels), BF16),
                pltpu.VMEM((1, channels), F32),
                pltpu.VMEM((channels, TAPS * channels), BF16),
                pltpu.VMEM((1, channels), F32),
                pltpu.VMEM((4, channels), BF16),
                pltpu.VMEM((1, 4), F32),
                pltpu.VMEM((4, CELLS), BF16),
                dma((8,)),
                dma((3, 6)),
                dma((3, 6)),
                dma((2, nr)),
                dma((2, nr)),
                dma((CHUNKS,)),
                dma((nb,)),
                dma((nb,)),
                dma((CHUNKS,)),
                dma((nr, CHUNKS)),
                dma((nr, CHUNKS)),
            ],
            compiler_params=pltpu.CompilerParams(
                collective_id=0, has_side_effects=True, vmem_limit_bytes=60 * 1024 * 1024
            ),
            cost_estimate=pl.CostEstimate(flops=360_000_000, bytes_accessed=2_000_000, transcendentals=65536),
        )(
            mic.reshape(1, CELLS),
            tissue,
            neighbours.reshape(1, 26),
            w1.T,
            b1.reshape(1, channels),
            w2,
            b2.reshape(1, channels),
            hw,
            hb.reshape(1, 4),
            cot.reshape(4, CELLS),
        )
        pred, gw1, gb1, gw2, gb2, gwh, gbh = pl.pallas_call(
            finish,
            out_shape=(
                jax.ShapeDtypeStruct((4, CELLS), BF16),
                jax.ShapeDtypeStruct((TAPS, channels), F32),
                jax.ShapeDtypeStruct((1, channels), F32),
                jax.ShapeDtypeStruct((channels, TAPS * channels), F32),
                jax.ShapeDtypeStruct((1, channels), F32),
                jax.ShapeDtypeStruct((4, channels), F32),
                jax.ShapeDtypeStruct((1, 4), F32),
            ),
            in_specs=[vmem] * 2,
            out_specs=(vmem,) * 7,
            compiler_params=pltpu.CompilerParams(vmem_limit_bytes=60 * 1024 * 1024),
        )(outs[1], outs[0])
        return (
            pred.reshape(1, 1, 4, CELLS),
            gw1.T,
            gb1.reshape(channels),
            gw2,
            gb2.reshape(channels),
            gwh,
            gbh.reshape(4),
        )

    return jax.shard_map(
        shards,
        mesh=mesh,
        in_specs=(
            P("region", "brick", None),
            P("region", "brick"),
            P("region", "brick", None),
            P(),
            P(),
            P(),
            P(),
            P(),
            P(),
            P("region", "brick", None, None),
        ),
        out_specs=(P("region", "brick", None, None), P(), P(), P(), P(), P(), P()),
        check_vma=False,
    )
```

```python
import functools
import math

import jax
import jax.numpy as jnp
from jax import lax
from jax.experimental import pallas as pl
from jax.experimental.pallas import tpu as pltpu
from jax.sharding import PartitionSpec as P

F32 = jnp.float32
BF16 = jnp.bfloat16
MESH = pl.DeviceIdType.MESH
TAPS = 27
PLANE = 64
CELLS = 512
WIDE = 640
DELTAS = (-3, -2, -1, 1, 2, 3)
CHUNKS = 8
CHUNK = 256
MAIN = 7 * CHUNK
MIC_ROWS = 32
SLOPE = math.sqrt(2 / math.pi)
CUBIC = 0.044715


def direction_id(a, c):
    full = (a + 1) * 9 + 3 + (c + 1)
    return full if full < 13 else full - 1


def iota(shape, dim):
    return lax.broadcasted_iota(jnp.int32, shape, dim)


def dot(left, right):
    return lax.dot_general(left, right, (((1,), (0,)), ((), ())), preferred_element_type=F32)


def dot_nt(left, right):
    return lax.dot_general(left, right, (((1,), (1,)), ((), ())), preferred_element_type=F32)


def column(row):
    size = row.shape[1]
    wide = jnp.broadcast_to(row, (size, size))
    return jnp.sum(jnp.where(iota((size, size), 0) == iota((size, size), 1), wide, 0.0), axis=1, keepdims=True)


def gelu_parts(values):
    square = values * values
    bent = jnp.tanh(SLOPE * (values + CUBIC * square * values))
    half = 0.5 * (1.0 + bent)
    slope = half + 0.5 * values * (1.0 - bent * bent) * (SLOPE * (1.0 + 3.0 * CUBIC * square))
    return values * half, slope


def halves(values):
    high = values.astype(BF16)
    return jnp.concatenate([high, (values - high.astype(F32)).astype(BF16)], axis=1)


def joined(pair):
    return pair[:, :128].astype(F32) + pair[:, 128:].astype(F32)


def for_each(count, body):
    if count <= 8:
        for step in range(count):
            body(step)
    else:
        def step_body(step, carry):
            body(step)
            return carry

        lax.fori_loop(0, count, step_body, 0)


def pack(field, pick, packet):
    rows = field.shape[0]
    low = iota((rows, 128), 1) < PLANE
    packet[0] = dot(field.astype(BF16), pick).astype(BF16)
    packet[1] = jnp.where(low, field[:, :128], field[:, CELLS - 128 :]).astype(BF16)


def widen(field, box, flags, spread):
    rows = field.shape[0]
    lane = iota((rows, 128), 1)
    m3, m2, m1, p1, p2, p3 = [box[k].astype(F32) for k in range(6)]
    ends = jnp.where(lane < PLANE, p2 * flags[1, 0], m2 * flags[-1, 0])
    padded = pltpu.roll(jnp.concatenate([field, ends], axis=1), 64, 1)
    first, inner, last = lane < 8, lane < 72, lane < 80
    above = jnp.where(
        first,
        pltpu.roll(m1, 72, 1) * flags[-1, 1],
        jnp.where(
            inner,
            pltpu.roll(p1, 8, 1) * flags[0, 1],
            jnp.where(last, pltpu.roll(p3, 72, 1) * flags[1, 1], 0.0),
        ),
    )
    below = jnp.where(
        first,
        pltpu.roll(m3, 8, 1) * flags[-1, -1],
        jnp.where(
            inner,
            pltpu.roll(m1, 72, 1) * flags[0, -1],
            jnp.where(last, pltpu.roll(p1, 8, 1) * flags[1, -1], 0.0),
        ),
    )
    halo = dot(jnp.concatenate([above, below], axis=1).astype(BF16), spread)
    return padded, halo


def windows(padded, halo, emit):
    row = iota((1, WIDE), 1)
    z = jnp.broadcast_to(row & 7, padded.shape)
    y = jnp.broadcast_to(row & 56, padded.shape)
    for c in (-1, 0, 1):
        if c == 0:
            along = padded
        elif c == 1:
            along = jnp.where(z == 7, halo, pltpu.roll(padded, WIDE - 1, 1))
        else:
            along = jnp.where(z == 0, halo, pltpu.roll(padded, 1, 1))
        emit(3 + c + 1, along)
        emit(c + 1, jnp.where(y == 0, 0.0, pltpu.roll(along, 8, 1)))
        emit(6 + c + 1, jnp.where(y == 56, 0.0, pltpu.roll(along, WIDE - 8, 1)))


def kernel(
    nb,
    nr,
    total_bricks,
    mic_hbm,
    tis_ref,
    nei_ref,
    w1_hbm,
    b1_hbm,
    w2_hbm,
    b2_hbm,
    hw_hbm,
    hb_hbm,
    cot_hbm,
    pred_out,
    fin_out,
    pred_ref,
    fin_ref,
    few_ref,
    s1_ref,
    s2_ref,
    w1p_ref,
    w2p_ref,
    front_ref,
    back_ref,
    a_ref,
    pick_ref,
    spread_ref,
    mic_out,
    h1_out,
    dz_out,
    mic_box,
    h1_box,
    dz_box,
    grad_ref,
    ra_ref,
    rb_src,
    rb_ref,
    mic_ref,
    w1_ref,
    b1_ref,
    w2_ref,
    b2_ref,
    hw_ref,
    hb_ref,
    cot_ref,
    in_sem,
    out_sem,
    few_send,
    few_recv,
    ex_send,
    ex_recv,
    a_send,
    a_recv,
    b_send,
    b_recv,
    gb_send,
    gb_recv,
    ga_send,
    ga_recv,
):
    me = lax.axis_index("brick")
    mr = lax.axis_index("region")
    channels = w2_ref.shape[0]
    rows = channels // nr

    sources = (mic_hbm, w1_hbm, b1_hbm, w2_hbm, b2_hbm, hw_hbm, hb_hbm, cot_hbm)
    places = (mic_ref, w1_ref, b1_ref, w2_ref, b2_ref, hw_ref, hb_ref, cot_ref)
    fetches = [
        pltpu.make_async_copy(source, place, in_sem.at[k])
        for k, (source, place) in enumerate(zip(sources, places))
    ]
    fetches[0].start()
    for box in (mic_box, h1_box, dz_box):
        box[...] = jnp.zeros_like(box)

    barrier = pltpu.get_barrier_semaphore()

    def greet_brick(step):
        pl.semaphore_signal(
            barrier, inc=1, device_id={"brick": (me + 1 + step) % nb}, device_id_type=MESH
        )

    for_each(nb - 1, greet_brick)
    for step in range(nr - 1):
        pl.semaphore_signal(
            barrier, inc=1, device_id={"region": (mr + 1 + step) % nr}, device_id_type=MESH
        )

    for fetch in fetches[1:]:
        fetch.start()

    spot, slot = iota((CELLS, 128), 0), iota((CELLS, 128), 1)
    pick_ref[...] = jnp.where(
        spot == (slot & 63) * 8 + 7 * (slot >> 6), 1.0, 0.0
    ).astype(BF16)
    pick = pick_ref[...]
    fetches[0].wait()
    mic = jnp.broadcast_to(mic_ref[...].astype(F32), (MIC_ROWS, CELLS))
    pack(mic, pick, mic_out)

    def exchange(index, packet, box, act):
        for k, delta in enumerate(DELTAS):
            back = DELTAS.index(-delta)
            other = me + delta

            @pl.when((other >= 0) & (other < nb))
            def _():
                if act == "recv":
                    copy = pltpu.make_async_remote_copy(
                        src_ref=packet.at[1 if abs(delta) == 2 else 0],
                        dst_ref=box.at[k],
                        send_sem=ex_send.at[index, k],
                        recv_sem=ex_recv.at[index, k],
                        device_id={"brick": other},
                        device_id_type=MESH,
                    )
                    copy.wait_recv()
                else:
                    copy = pltpu.make_async_remote_copy(
                        src_ref=packet.at[1 if abs(delta) == 2 else 0],
                        dst_ref=box.at[back],
                        send_sem=ex_send.at[index, k],
                        recv_sem=ex_recv.at[index, back],
                        device_id={"brick": other},
                        device_id_type=MESH,
                    )
                    if act == "start":
                        copy.start()
                    else:
                        copy.wait_send()

    pl.semaphore_wait(barrier, nb - 1 + nr - 1)
    exchange(0, mic_out, mic_box, "start")

    spread_row, spread_lane = iota((256, WIDE), 0), iota((256, WIDE), 1)
    spread_ref[...] = jnp.where(
        spread_lane == (spread_row & 127) * 8 + 7 - 7 * (spread_row >> 7), 1.0, 0.0
    ).astype(BF16)
    for fetch in fetches[1:]:
        fetch.wait()
    w1p_ref[...] = jnp.zeros_like(w1p_ref)
    w1p_ref[:TAPS, :] = w1_ref[...]
    s1_ref[9 * channels :, :] = jnp.zeros((channels, WIDE), BF16)
    s2_ref[9 * channels :, :] = jnp.zeros((channels, WIDE), BF16)
    w2p_ref[:, MAIN - 128 :] = jnp.zeros((channels, 128), BF16)
    w2p_ref[:, : TAPS * channels] = w2_ref[...]
    taps_lane = iota((channels, WIDE), 1) < 9 * channels
    for a in range(3):
        view = w2p_ref[:, 512 * a + 64 * a - 64 * (a % 2) : 512 * a + 64 * a - 64 * (a % 2) + WIDE]
        if a % 2:
            view = pltpu.roll(view.astype(F32), WIDE - 64, 1)
        view = jnp.where(taps_lane, view.astype(F32), 0.0)
        front_ref[a * channels : (a + 1) * channels, :] = view.astype(BF16)
    flags = {}
    for a in (-1, 0, 1):
        for c in (-1, 0, 1):
            if (a, c) != (0, 0):
                flags[a, c] = jnp.where(nei_ref[0, direction_id(a, c)] >= 0, 1.0, 0.0).astype(F32)
    active = tis_ref[0, 0].astype(F32)
    bias1 = column(b1_ref[...])
    bias2 = column(b2_ref[...])
    bias3 = jnp.sum(
        jnp.where(iota((4, 4), 0) == iota((4, 4), 1), jnp.broadcast_to(hb_ref[...], (4, 4)), 0.0),
        axis=1,
        keepdims=True,
    )
    dpred = (cot_ref[...].astype(F32) * active / total_bricks).astype(BF16)
    dpred_wide = jnp.concatenate([dpred.astype(F32), jnp.zeros((4, CELLS), F32)], axis=0)
    d_second = lax.dot_general(
        hw_ref[...], dpred, (((0,), (0,)), ((), ())), preferred_element_type=F32
    )

    exchange(0, mic_out, mic_box, "recv")
    spread = spread_ref[...]
    padded, halo = widen(mic, mic_box, flags, spread)
    row = iota((MIC_ROWS, CELLS), 0)
    taps = [jnp.where((row >= 27) & (row < 30), 1.0, 0.0).astype(F32)]

    def emit_mic(index, value):
        rolled = pltpu.roll(value, WIDE - PLANE, 1)
        views = (value[:, :CELLS], rolled[:, :CELLS], value[:, 128:])
        for a in range(3):
            taps[0] = jnp.where(row == 9 * a + index, views[a], taps[0])

    windows(padded, halo, emit_mic)
    a_ref[...] = jnp.concatenate(
        [taps[0], dpred_wide, jnp.zeros((128 - MIC_ROWS - 8, CELLS), F32)], axis=0
    ).astype(BF16)
    z1 = (
        lax.dot_general(
            w1p_ref[...], a_ref[...], (((0,), (0,)), ((), ())), preferred_element_type=F32
        )
        + bias1
    )
    value1, slope1 = gelu_parts(z1)
    h1 = (value1 * active).astype(BF16).astype(F32)
    pack(h1, pick, h1_out)
    exchange(1, h1_out, h1_box, "start")
    slope1 = slope1 * active

    back = []
    for j in range(14):
        upper = w2p_ref[:, 128 * (13 - j) : 128 * (14 - j)].astype(F32)
        if j == 0:
            upper = jnp.where(iota((channels, 128), 1) < channels, upper, 0.0)
        if j < 13:
            lower = w2p_ref[:, 128 * (12 - j) : 128 * (13 - j)].astype(F32)
        else:
            lower = jnp.zeros((channels, 128), F32)
        turned = jnp.concatenate([upper, lower], axis=0).T
        back.append(
            jnp.where(iota((channels, 128), 1) < channels, turned[:channels], turned[channels:])
        )
    for a in range(3):
        first_tile = (9 * a) // 2
        view = jnp.concatenate(back[first_tile : first_tile + 5], axis=1)
        if a % 2:
            view = pltpu.roll(view, WIDE - 64, 1)
        view = jnp.where(taps_lane, view, 0.0)
        back_ref[a * channels : (a + 1) * channels, :] = view.astype(BF16)

    def store_windows(target):
        def emit(index, value):
            target[index * channels : (index + 1) * channels, :] = value.astype(BF16)

        return emit

    def convolve(weights, target):
        wide = dot(weights[...], target[...])
        middle = pltpu.roll(wide[channels : 2 * channels], WIDE - PLANE, 1)
        return (
            wide[:channels, :CELLS] + middle[:, :CELLS] + wide[2 * channels :, WIDE - CELLS :]
        )

    exchange(1, h1_out, h1_box, "recv")
    padded, halo = widen(h1, h1_box, flags, spread)
    windows(padded, halo, store_windows(s1_ref))
    z2 = convolve(front_ref, s1_ref) + bias2
    value2, slope2 = gelu_parts(z2)
    dz2 = (d_second * slope2 * active).astype(BF16)
    pack(dz2.astype(F32), pick, dz_out)
    exchange(2, dz_out, dz_box, "start")

    dz2_wide = dz2.astype(F32)
    gap = jnp.zeros((channels, 128), F32)
    left = jnp.concatenate([dz2_wide, gap], axis=1)
    stacked = jnp.concatenate(
        [left, pltpu.roll(left, PLANE, 1), jnp.concatenate([gap, dz2_wide], axis=1)], axis=0
    ).astype(BF16)
    grads = dot_nt(stacked, s1_ref[...])
    centre = pltpu.roll(grads[channels : 2 * channels], PLANE, 1)
    grad_ref[:, :512] = grads[:channels, :512].astype(BF16)
    grad_ref[:, 512:640] = (grads[:channels, 512:] + centre[:, :128]).astype(BF16)
    grad_ref[:, 640:1152] = centre[:, 128:].astype(BF16)
    grad_ref[:, 1152:MAIN] = grads[2 * channels :].astype(BF16)

    def region_copy(part, step, act):
        other = (mr + 1 + step) % nr
        lanes = pl.ds(0, MAIN) if part == 0 else pl.ds(MAIN, CHUNK)
        owner = other if act != "recv" else mr
        slot_id = mr if act != "recv" else other
        copy = pltpu.make_async_remote_copy(
            src_ref=grad_ref.at[pl.ds(pl.multiple_of(owner * rows, rows), rows), lanes],
            dst_ref=ra_ref.at[slot_id, :, lanes],
            send_sem=a_send.at[part, other],
            recv_sem=a_recv.at[part, slot_id],
            device_id={"region": other},
            device_id_type=MESH,
        )
        if act == "start":
            copy.start()
        elif act == "recv":
            copy.wait_recv()
        else:
            copy.wait_send()

    for step in range(nr - 1):
        region_copy(0, step, "start")

    h2 = (value2 * active).astype(BF16)
    linear = dot(hw_ref[...], h2) + bias3
    pred_ref[...] = (linear * active).astype(BF16)
    pred_copy = pltpu.make_async_copy(pred_ref, pred_out, out_sem.at[CHUNKS])
    pred_copy.start()
    tap_rows = a_ref[...]
    dpred_tall = jnp.concatenate(
        [dpred_wide, jnp.zeros((channels - 8, CELLS), F32)], axis=0
    ).astype(BF16)
    lane = iota((channels, 128), 1)
    small = jnp.where(lane == 28, dot_nt(dz2, tap_rows), 0.0)
    small = small + jnp.where((lane >= 32) & (lane < 36), dot_nt(h2, tap_rows), 0.0)
    small = small + jnp.where(lane == 29, dot_nt(dpred_tall, tap_rows), 0.0)

    def brick_copy(chunk, act):
        @pl.when(me != chunk)
        def _():
            copy = pltpu.make_async_remote_copy(
                src_ref=rb_src.at[chunk],
                dst_ref=rb_ref.at[me],
                send_sem=b_send.at[chunk],
                recv_sem=b_recv.at[me],
                device_id={"brick": chunk},
                device_id_type=MESH,
            )
            if act == "start":
                copy.start()
            else:
                copy.wait_send()

    mine = pl.ds(pl.multiple_of(mr * rows, rows), rows)

    def region_sum(part):
        lanes = pl.ds(0, MAIN) if part == 0 else pl.ds(MAIN, CHUNK)
        for step in range(nr - 1):
            region_copy(part, step, "recv")
        total = grad_ref[mine, lanes].astype(F32)
        for step in range(nr - 1):
            total = total + ra_ref[(mr + 1 + step) % nr, :, lanes].astype(F32)
        return total

    exchange(2, dz_out, dz_box, "recv")
    padded, halo = widen(dz2.astype(F32), dz_box, flags, spread)
    windows(padded, halo, store_windows(s2_ref))
    total = region_sum(0)
    for chunk in range(CHUNKS - 1):
        rb_src[chunk] = total[:, CHUNK * chunk : CHUNK * (chunk + 1)].astype(BF16)
        brick_copy(chunk, "start")
    dz1 = (convolve(back_ref, s2_ref) * slope1).astype(BF16)
    small = small + jnp.where(lane < 28, dot_nt(dz1, tap_rows), 0.0)
    grad_ref[:, MAIN:] = halves(small)
    for step in range(nr - 1):
        region_copy(1, step, "start")

    def gather_copy(step, act):
        other = (me + 1 + step) % nb
        copy = pltpu.make_async_remote_copy(
            src_ref=fin_ref.at[me % CHUNKS],
            dst_ref=fin_ref.at[me % CHUNKS],
            send_sem=gb_send.at[other],
            recv_sem=gb_recv.at[me % CHUNKS],
            device_id={"brick": other},
            device_id_type=MESH,
        )
        if act == "start":
            copy.start()
        else:
            copy.wait_send()

    def own():
        def arrived(step):
            other = (me + 1 + step) % nb
            pltpu.make_async_remote_copy(
                src_ref=rb_src.at[0],
                dst_ref=rb_ref.at[other],
                send_sem=b_send.at[0],
                recv_sem=b_recv.at[other],
                device_id={"brick": other},
                device_id_type=MESH,
            ).wait_recv()

        for_each(nb - 1, arrived)
        kept = rb_src[me % CHUNKS].astype(F32)
        if nb <= CHUNKS:
            for step in range(nb - 1):
                kept = kept + rb_ref[(me + 1 + step) % nb].astype(F32)
        else:
            kept = lax.fori_loop(
                0, nb - 1, lambda step, s: s + rb_ref[(me + 1 + step) % nb].astype(F32), kept
            )
        fin_ref[me % CHUNKS] = kept.astype(BF16)
        for_each(nb - 1, lambda step: gather_copy(step, "start"))

    def spread_copy(chunk, step, act):
        other = (mr + 1 + step) % nr
        slot_id = other if act == "recv" else mr
        copy = pltpu.make_async_remote_copy(
            src_ref=fin_ref.at[chunk],
            dst_ref=fin_out.at[slot_id, chunk],
            send_sem=ga_send.at[other, chunk],
            recv_sem=ga_recv.at[slot_id, chunk],
            device_id={"region": other},
            device_id_type=MESH,
        )
        if act == "start":
            copy.start()
        elif act == "recv":
            copy.wait_recv()
        else:
            copy.wait_send()

    pl.when(me < CHUNKS - 1)(own)

    def few_copy(step, act):
        other = (me + 1 + step) % nb
        slot_id = other if act == "recv" else me
        copy = pltpu.make_async_remote_copy(
            src_ref=rb_src.at[CHUNKS - 1],
            dst_ref=few_ref.at[slot_id],
            send_sem=few_send.at[other],
            recv_sem=few_recv.at[slot_id],
            device_id={"brick": other},
            device_id_type=MESH,
        )
        if act == "start":
            copy.start()
        elif act == "recv":
            copy.wait_recv()
        else:
            copy.wait_send()

    few = halves(joined(region_sum(1)))
    rb_src[CHUNKS - 1] = few
    for_each(nb - 1, lambda step: few_copy(step, "start"))
    few_ref[me] = few

    def keep(chunk):
        return pltpu.make_async_copy(fin_ref.at[chunk], fin_out.at[mr, chunk], out_sem.at[chunk])

    def pass_on(chunk):
        for step in range(nr - 1):
            spread_copy(chunk, step, "start")
        keep(chunk).start()

    for chunk in range(CHUNKS - 1):
        @pl.when(me != chunk)
        def _():
            pltpu.make_async_remote_copy(
                src_ref=fin_ref.at[chunk],
                dst_ref=fin_ref.at[chunk],
                send_sem=gb_send.at[chunk],
                recv_sem=gb_recv.at[chunk],
                device_id={"brick": chunk},
                device_id_type=MESH,
            ).wait_recv()

        pass_on(chunk)

    for_each(nb - 1, lambda step: few_copy(step, "recv"))
    if nb <= CHUNKS:
        few = joined(few_ref[0])
        for brick in range(1, nb):
            few = few + joined(few_ref[brick])
    else:
        few = lax.fori_loop(1, nb, lambda brick, s: s + joined(few_ref[brick]), joined(few_ref[0]))
    fin_ref[CHUNKS - 1] = halves(few)
    pass_on(CHUNKS - 1)

    exchange(0, mic_out, mic_box, "sent")
    exchange(1, h1_out, h1_box, "sent")
    exchange(2, dz_out, dz_box, "sent")
    for part in range(2):
        for step in range(nr - 1):
            region_copy(part, step, "sent")
    for chunk in range(CHUNKS - 1):
        brick_copy(chunk, "sent")
    pl.when(me < CHUNKS - 1)(lambda: for_each(nb - 1, lambda step: gather_copy(step, "sent")))
    for_each(nb - 1, lambda step: few_copy(step, "sent"))
    pred_copy.wait()
    for chunk in range(CHUNKS):
        keep(chunk).wait()
    for chunk in range(CHUNKS):
        for step in range(nr - 1):
            spread_copy(chunk, step, "recv")
            spread_copy(chunk, step, "sent")


def finish(
    fin_ref, raw_ref, pred_ref, gw1_ref, gb1_ref, gw2_ref, gb2_ref, gwh_ref, gbh_ref
):
    nr, _, rows, _ = fin_ref.shape
    channels = nr * rows
    pred_ref[...] = raw_ref[...]
    for region in range(nr):
        where = slice(region * rows, (region + 1) * rows)
        for chunk in range(CHUNKS - 1):
            block = fin_ref[region, chunk].astype(F32)
            if chunk < CHUNKS - 2:
                gw2_ref[where, CHUNK * chunk : CHUNK * (chunk + 1)] = block
            else:
                gw2_ref[where, CHUNK * chunk : CHUNK * chunk + 128] = block[:, :128]
                gw2_ref[where, CHUNK * chunk + 128 : TAPS * channels] = block[
                    :, 128 : TAPS * channels - CHUNK * chunk
                ]
    small = jnp.concatenate(
        [joined(fin_ref[region, CHUNKS - 1]) for region in range(nr)], axis=0
    )
    turned = jnp.concatenate([small, jnp.zeros((128 - channels, 128), F32)], axis=0).T
    gw1_ref[...] = turned[:TAPS, :channels]
    gb1_ref[...] = turned[27:28, :channels]
    gb2_ref[...] = turned[28:29, :channels]
    gbh_ref[...] = turned[29:30, :4]
    gwh_ref[...] = turned[32:36, :channels]


def solution(mesh):
    nb, nr = mesh.shape["brick"], mesh.shape["region"]

    def shards(mic, tissue, neighbours, w1, b1, w2, b2, hw, hb, cot):
        channels = w1.shape[0]
        rows = channels // nr
        vmem = pl.BlockSpec(memory_space=pltpu.VMEM)
        hbm = pl.BlockSpec(memory_space=pl.ANY)
        smem = pl.BlockSpec(memory_space=pltpu.SMEM)
        dma = pltpu.SemaphoreType.DMA
        total_bricks = nb * nr * mic.shape[1]
        outs = pl.pallas_call(
            functools.partial(kernel, nb, nr, total_bricks),
            out_shape=(
                jax.ShapeDtypeStruct((4, CELLS), BF16),
                jax.ShapeDtypeStruct((nr, CHUNKS, rows, CHUNK), BF16),
            ),
            in_specs=[hbm, smem, smem] + [hbm] * 7,
            out_specs=(hbm,) * 2,
            scratch_shapes=[
                pltpu.VMEM((4, CELLS), BF16),
                pltpu.VMEM((CHUNKS, rows, CHUNK), BF16),
                pltpu.VMEM((nb, rows, CHUNK), BF16),
                pltpu.VMEM((WIDE, WIDE), BF16),
                pltpu.VMEM((WIDE, WIDE), BF16),
                pltpu.VMEM((128, channels), BF16),
                pltpu.VMEM((channels, MAIN), BF16),
                pltpu.VMEM((3 * channels, WIDE), BF16),
                pltpu.VMEM((3 * channels, WIDE), BF16),
                pltpu.VMEM((128, CELLS), BF16),
                pltpu.VMEM((CELLS, 128), BF16),
                pltpu.VMEM((256, WIDE), BF16),
                pltpu.VMEM((2, MIC_ROWS, 128), BF16),
                pltpu.VMEM((2, channels, 128), BF16),
                pltpu.VMEM((2, channels, 128), BF16),
                pltpu.VMEM((6, MIC_ROWS, 128), BF16),
                pltpu.VMEM((6, channels, 128), BF16),
                pltpu.VMEM((6, channels, 128), BF16),
                pltpu.VMEM((channels, MAIN + CHUNK), BF16),
                pltpu.VMEM((nr, rows, MAIN + CHUNK), BF16),
                pltpu.VMEM((CHUNKS, rows, CHUNK), BF16),
                pltpu.VMEM((nb, rows, CHUNK), BF16),
                pltpu.VMEM((1, CELLS), BF16),
                pltpu.VMEM((TAPS, channels), BF16),
                pltpu.VMEM((1, channels), F32),
                pltpu.VMEM((channels, TAPS * channels), BF16),
                pltpu.VMEM((1, channels), F32),
                pltpu.VMEM((4, channels), BF16),
                pltpu.VMEM((1, 4), F32),
                pltpu.VMEM((4, CELLS), BF16),
                dma((8,)),
                dma((CHUNKS + 1,)),
                dma((nb,)),
                dma((nb,)),
                dma((3, 6)),
                dma((3, 6)),
                dma((2, nr)),
                dma((2, nr)),
                dma((CHUNKS,)),
                dma((nb,)),
                dma((nb,)),
                dma((CHUNKS,)),
                dma((nr, CHUNKS)),
                dma((nr, CHUNKS)),
            ],
            compiler_params=pltpu.CompilerParams(
                collective_id=0, has_side_effects=True, vmem_limit_bytes=60 * 1024 * 1024
            ),
            cost_estimate=pl.CostEstimate(flops=360_000_000, bytes_accessed=2_000_000, transcendentals=65536),
        )(
            mic.reshape(1, CELLS),
            tissue,
            neighbours.reshape(1, 26),
            w1.T,
            b1.reshape(1, channels),
            w2,
            b2.reshape(1, channels),
            hw,
            hb.reshape(1, 4),
            cot.reshape(4, CELLS),
        )
        pred, gw1, gb1, gw2, gb2, gwh, gbh = pl.pallas_call(
            finish,
            out_shape=(
                jax.ShapeDtypeStruct((4, CELLS), BF16),
                jax.ShapeDtypeStruct((TAPS, channels), F32),
                jax.ShapeDtypeStruct((1, channels), F32),
                jax.ShapeDtypeStruct((channels, TAPS * channels), F32),
                jax.ShapeDtypeStruct((1, channels), F32),
                jax.ShapeDtypeStruct((4, channels), F32),
                jax.ShapeDtypeStruct((1, 4), F32),
            ),
            in_specs=[vmem] * 2,
            out_specs=(vmem,) * 7,
            compiler_params=pltpu.CompilerParams(vmem_limit_bytes=60 * 1024 * 1024),
        )(outs[1], outs[0])
        return (
            pred.reshape(1, 1, 4, CELLS),
            gw1.T,
            gb1.reshape(channels),
            gw2,
            gb2.reshape(channels),
            gwh,
            gbh.reshape(4),
        )

    return jax.shard_map(
        shards,
        mesh=mesh,
        in_specs=(
            P("region", "brick", None),
            P("region", "brick"),
            P("region", "brick", None),
            P(),
            P(),
            P(),
            P(),
            P(),
            P(),
            P("region", "brick", None, None),
        ),
        out_specs=(P("region", "brick", None, None), P(), P(), P(), P(), P(), P()),
        check_vma=False,
    )
```

```python
import functools
import math

import jax
import jax.numpy as jnp
from jax import lax
from jax.experimental import pallas as pl
from jax.experimental.pallas import tpu as pltpu
from jax.sharding import PartitionSpec as P

F32 = jnp.float32
BF16 = jnp.bfloat16
MESH = pl.DeviceIdType.MESH
TAPS = 27
PLANE = 64
CELLS = 512
WIDE = 640
DELTAS = (-3, -2, -1, 1, 2, 3)
CHUNKS = 8
CHUNK = 256
MAIN = 7 * CHUNK
MIC_ROWS = 32
SLOPE = math.sqrt(2 / math.pi)
CUBIC = 0.044715


def direction_id(a, c):
    full = (a + 1) * 9 + 3 + (c + 1)
    return full if full < 13 else full - 1


def iota(shape, dim):
    return lax.broadcasted_iota(jnp.int32, shape, dim)


def dot(left, right):
    return lax.dot_general(left, right, (((1,), (0,)), ((), ())), preferred_element_type=F32)


def dot_nt(left, right):
    return lax.dot_general(left, right, (((1,), (1,)), ((), ())), preferred_element_type=F32)


def column(row):
    size = row.shape[1]
    wide = jnp.broadcast_to(row, (size, size))
    return jnp.sum(jnp.where(iota((size, size), 0) == iota((size, size), 1), wide, 0.0), axis=1, keepdims=True)


def gelu_parts(values):
    square = values * values
    bent = jnp.tanh(SLOPE * (values + CUBIC * square * values))
    half = 0.5 * (1.0 + bent)
    slope = half + 0.5 * values * (1.0 - bent * bent) * (SLOPE * (1.0 + 3.0 * CUBIC * square))
    return values * half, slope


def halves(values):
    high = values.astype(BF16)
    return jnp.concatenate([high, (values - high.astype(F32)).astype(BF16)], axis=1)


def joined(pair):
    return pair[:, :128].astype(F32) + pair[:, 128:].astype(F32)


def for_each(count, body):
    if count <= 8:
        for step in range(count):
            body(step)
    else:
        def step_body(step, carry):
            body(step)
            return carry

        lax.fori_loop(0, count, step_body, 0)


def pack(field, pick, packet):
    rows = field.shape[0]
    low = iota((rows, 128), 1) < PLANE
    packet[0] = dot(field.astype(BF16), pick).astype(BF16)
    packet[1] = jnp.where(low, field[:, :128], field[:, CELLS - 128 :]).astype(BF16)


def widen(field, box, flags, spread):
    rows = field.shape[0]
    lane = iota((rows, 128), 1)
    m3, m2, m1, p1, p2, p3 = [box[k].astype(F32) for k in range(6)]
    ends = jnp.where(lane < PLANE, p2 * flags[1, 0], m2 * flags[-1, 0])
    padded = pltpu.roll(jnp.concatenate([field, ends], axis=1), 64, 1)
    first, inner, last = lane < 8, lane < 72, lane < 80
    above = jnp.where(
        first,
        pltpu.roll(m1, 72, 1) * flags[-1, 1],
        jnp.where(
            inner,
            pltpu.roll(p1, 8, 1) * flags[0, 1],
            jnp.where(last, pltpu.roll(p3, 72, 1) * flags[1, 1], 0.0),
        ),
    )
    below = jnp.where(
        first,
        pltpu.roll(m3, 8, 1) * flags[-1, -1],
        jnp.where(
            inner,
            pltpu.roll(m1, 72, 1) * flags[0, -1],
            jnp.where(last, pltpu.roll(p1, 8, 1) * flags[1, -1], 0.0),
        ),
    )
    halo = dot(jnp.concatenate([above, below], axis=1).astype(BF16), spread)
    return padded, halo


def windows(padded, halo, emit):
    row = iota((1, WIDE), 1)
    z = jnp.broadcast_to(row & 7, padded.shape)
    y = jnp.broadcast_to(row & 56, padded.shape)
    for c in (-1, 0, 1):
        if c == 0:
            along = padded
        elif c == 1:
            along = jnp.where(z == 7, halo, pltpu.roll(padded, WIDE - 1, 1))
        else:
            along = jnp.where(z == 0, halo, pltpu.roll(padded, 1, 1))
        emit(3 + c + 1, along)
        emit(c + 1, jnp.where(y == 0, 0.0, pltpu.roll(along, 8, 1)))
        emit(6 + c + 1, jnp.where(y == 56, 0.0, pltpu.roll(along, WIDE - 8, 1)))


def kernel(
    nb,
    nr,
    total_bricks,
    mic_hbm,
    tis_ref,
    nei_ref,
    w1_hbm,
    b1_hbm,
    w2_hbm,
    b2_hbm,
    hw_hbm,
    hb_hbm,
    cot_hbm,
    pred_out,
    fin_out,
    pred_ref,
    fin_ref,
    few_ref,
    s1_ref,
    s2_ref,
    w1p_ref,
    w2p_ref,
    front_ref,
    back_ref,
    a_ref,
    pick_ref,
    spread_ref,
    mic_out,
    h1_out,
    dz_out,
    mic_box,
    h1_box,
    dz_box,
    grad_ref,
    ra_ref,
    rb_src,
    rb_ref,
    mic_ref,
    w1_ref,
    b1_ref,
    w2_ref,
    b2_ref,
    hw_ref,
    hb_ref,
    cot_ref,
    in_sem,
    out_sem,
    few_send,
    few_recv,
    ex_send,
    ex_recv,
    a_send,
    a_recv,
    b_send,
    b_recv,
    gb_send,
    gb_recv,
    ga_send,
    ga_recv,
):
    me = lax.axis_index("brick")
    mr = lax.axis_index("region")
    channels = w2_ref.shape[0]
    rows = channels // nr

    sources = (mic_hbm, w1_hbm, b1_hbm, w2_hbm, b2_hbm, hw_hbm, hb_hbm, cot_hbm)
    places = (mic_ref, w1_ref, b1_ref, w2_ref, b2_ref, hw_ref, hb_ref, cot_ref)
    fetches = [
        pltpu.make_async_copy(source, place, in_sem.at[k])
        for k, (source, place) in enumerate(zip(sources, places))
    ]
    fetches[0].start()
    for box in (mic_box, h1_box, dz_box):
        box[...] = jnp.zeros_like(box)

    barrier = pltpu.get_barrier_semaphore()

    def greet_brick(step):
        pl.semaphore_signal(
            barrier, inc=1, device_id={"brick": (me + 1 + step) % nb}, device_id_type=MESH
        )

    for_each(nb - 1, greet_brick)
    for step in range(nr - 1):
        pl.semaphore_signal(
            barrier, inc=1, device_id={"region": (mr + 1 + step) % nr}, device_id_type=MESH
        )

    for fetch in fetches[1:]:
        fetch.start()

    spot, slot = iota((CELLS, 128), 0), iota((CELLS, 128), 1)
    pick_ref[...] = jnp.where(
        spot == (slot & 63) * 8 + 7 * (slot >> 6), 1.0, 0.0
    ).astype(BF16)
    pick = pick_ref[...]
    fetches[0].wait()
    mic = jnp.broadcast_to(mic_ref[...].astype(F32), (MIC_ROWS, CELLS))
    pack(mic, pick, mic_out)

    def exchange(index, packet, box, act):
        for k, delta in enumerate(DELTAS):
            back = DELTAS.index(-delta)
            other = me + delta

            @pl.when((other >= 0) & (other < nb))
            def _():
                if act == "recv":
                    copy = pltpu.make_async_remote_copy(
                        src_ref=packet.at[1 if abs(delta) == 2 else 0],
                        dst_ref=box.at[k],
                        send_sem=ex_send.at[index, k],
                        recv_sem=ex_recv.at[index, k],
                        device_id={"brick": other},
                        device_id_type=MESH,
                    )
                    copy.wait_recv()
                else:
                    copy = pltpu.make_async_remote_copy(
                        src_ref=packet.at[1 if abs(delta) == 2 else 0],
                        dst_ref=box.at[back],
                        send_sem=ex_send.at[index, k],
                        recv_sem=ex_recv.at[index, back],
                        device_id={"brick": other},
                        device_id_type=MESH,
                    )
                    if act == "start":
                        copy.start()
                    else:
                        copy.wait_send()

    pl.semaphore_wait(barrier, nb - 1 + nr - 1)
    exchange(0, mic_out, mic_box, "start")

    spread_row, spread_lane = iota((256, WIDE), 0), iota((256, WIDE), 1)
    spread_ref[...] = jnp.where(
        spread_lane == (spread_row & 127) * 8 + 7 - 7 * (spread_row >> 7), 1.0, 0.0
    ).astype(BF16)
    for fetch in fetches[1:]:
        fetch.wait()
    w1p_ref[...] = jnp.zeros_like(w1p_ref)
    w1p_ref[:TAPS, :] = w1_ref[...]
    s1_ref[9 * channels :, :] = jnp.zeros((channels, WIDE), BF16)
    s2_ref[9 * channels :, :] = jnp.zeros((channels, WIDE), BF16)
    w2p_ref[:, MAIN - 128 :] = jnp.zeros((channels, 128), BF16)
    w2p_ref[:, : TAPS * channels] = w2_ref[...]
    taps_lane = iota((channels, WIDE), 1) < 9 * channels
    for a in range(3):
        view = w2p_ref[:, 512 * a + 64 * a - 64 * (a % 2) : 512 * a + 64 * a - 64 * (a % 2) + WIDE]
        if a % 2:
            view = pltpu.roll(view.astype(F32), WIDE - 64, 1)
        view = jnp.where(taps_lane, view.astype(F32), 0.0)
        front_ref[a * channels : (a + 1) * channels, :] = view.astype(BF16)
    flags = {}
    for a in (-1, 0, 1):
        for c in (-1, 0, 1):
            if (a, c) != (0, 0):
                flags[a, c] = jnp.where(nei_ref[0, direction_id(a, c)] >= 0, 1.0, 0.0).astype(F32)
    active = tis_ref[0, 0].astype(F32)
    bias1 = column(b1_ref[...])
    bias2 = column(b2_ref[...])
    bias3 = jnp.sum(
        jnp.where(iota((4, 4), 0) == iota((4, 4), 1), jnp.broadcast_to(hb_ref[...], (4, 4)), 0.0),
        axis=1,
        keepdims=True,
    )
    dpred = (cot_ref[...].astype(F32) * active / total_bricks).astype(BF16)
    dpred_wide = jnp.concatenate([dpred.astype(F32), jnp.zeros((4, CELLS), F32)], axis=0)
    d_second = lax.dot_general(
        hw_ref[...], dpred, (((0,), (0,)), ((), ())), preferred_element_type=F32
    )

    exchange(0, mic_out, mic_box, "recv")
    spread = spread_ref[...]
    padded, halo = widen(mic, mic_box, flags, spread)
    row = iota((MIC_ROWS, CELLS), 0)
    taps = [jnp.where((row >= 27) & (row < 30), 1.0, 0.0).astype(F32)]

    def emit_mic(index, value):
        rolled = pltpu.roll(value, WIDE - PLANE, 1)
        views = (value[:, :CELLS], rolled[:, :CELLS], value[:, 128:])
        for a in range(3):
            taps[0] = jnp.where(row == 9 * a + index, views[a], taps[0])

    windows(padded, halo, emit_mic)
    a_ref[...] = jnp.concatenate(
        [taps[0], dpred_wide, jnp.zeros((128 - MIC_ROWS - 8, CELLS), F32)], axis=0
    ).astype(BF16)
    z1 = (
        lax.dot_general(
            w1p_ref[...], a_ref[...], (((0,), (0,)), ((), ())), preferred_element_type=F32
        )
        + bias1
    )
    value1, slope1 = gelu_parts(z1)
    h1 = (value1 * active).astype(BF16).astype(F32)
    pack(h1, pick, h1_out)
    exchange(1, h1_out, h1_box, "start")
    slope1 = slope1 * active

    back = []
    for j in range(14):
        upper = w2p_ref[:, 128 * (13 - j) : 128 * (14 - j)].astype(F32)
        if j == 0:
            upper = jnp.where(iota((channels, 128), 1) < channels, upper, 0.0)
        if j < 13:
            lower = w2p_ref[:, 128 * (12 - j) : 128 * (13 - j)].astype(F32)
        else:
            lower = jnp.zeros((channels, 128), F32)
        turned = jnp.concatenate([upper, lower], axis=0).T
        back.append(
            jnp.where(iota((channels, 128), 1) < channels, turned[:channels], turned[channels:])
        )
    for a in range(3):
        first_tile = (9 * a) // 2
        view = jnp.concatenate(back[first_tile : first_tile + 5], axis=1)
        if a % 2:
            view = pltpu.roll(view, WIDE - 64, 1)
        view = jnp.where(taps_lane, view, 0.0)
        back_ref[a * channels : (a + 1) * channels, :] = view.astype(BF16)

    def store_windows(target):
        def emit(index, value):
            target[index * channels : (index + 1) * channels, :] = value.astype(BF16)

        return emit

    def convolve(weights, target):
        wide = dot(weights[...], target[...])
        middle = pltpu.roll(wide[channels : 2 * channels], WIDE - PLANE, 1)
        return (
            wide[:channels, :CELLS] + middle[:, :CELLS] + wide[2 * channels :, WIDE - CELLS :]
        )

    exchange(1, h1_out, h1_box, "recv")
    padded, halo = widen(h1, h1_box, flags, spread)
    windows(padded, halo, store_windows(s1_ref))
    z2 = convolve(front_ref, s1_ref) + bias2
    value2, slope2 = gelu_parts(z2)
    dz2 = (d_second * slope2 * active).astype(BF16)
    pack(dz2.astype(F32), pick, dz_out)
    exchange(2, dz_out, dz_box, "start")

    dz2_wide = dz2.astype(F32)
    gap = jnp.zeros((channels, 128), F32)
    left = jnp.concatenate([dz2_wide, gap], axis=1)
    stacked = jnp.concatenate(
        [left, pltpu.roll(left, PLANE, 1), jnp.concatenate([gap, dz2_wide], axis=1)], axis=0
    ).astype(BF16)
    grads = dot_nt(stacked, s1_ref[...])
    centre = pltpu.roll(grads[channels : 2 * channels], PLANE, 1)
    grad_ref[:, :512] = grads[:channels, :512].astype(BF16)
    grad_ref[:, 512:640] = (grads[:channels, 512:] + centre[:, :128]).astype(BF16)
    grad_ref[:, 640:1152] = centre[:, 128:].astype(BF16)
    grad_ref[:, 1152:MAIN] = grads[2 * channels :].astype(BF16)

    def region_copy(part, step, act):
        other = (mr + 1 + step) % nr
        lanes = pl.ds(0, MAIN) if part == 0 else pl.ds(MAIN, CHUNK)
        owner = other if act != "recv" else mr
        slot_id = mr if act != "recv" else other
        copy = pltpu.make_async_remote_copy(
            src_ref=grad_ref.at[pl.ds(pl.multiple_of(owner * rows, rows), rows), lanes],
            dst_ref=ra_ref.at[slot_id, :, lanes],
            send_sem=a_send.at[part, other],
            recv_sem=a_recv.at[part, slot_id],
            device_id={"region": other},
            device_id_type=MESH,
        )
        if act == "start":
            copy.start()
        elif act == "recv":
            copy.wait_recv()
        else:
            copy.wait_send()

    for step in range(nr - 1):
        region_copy(0, step, "start")

    h2 = (value2 * active).astype(BF16)
    linear = dot(hw_ref[...], h2) + bias3
    pred_ref[...] = (linear * active).astype(BF16)
    pred_copy = pltpu.make_async_copy(pred_ref, pred_out, out_sem.at[CHUNKS])
    pred_copy.start()
    tap_rows = a_ref[...]
    dpred_tall = jnp.concatenate(
        [dpred_wide, jnp.zeros((channels - 8, CELLS), F32)], axis=0
    ).astype(BF16)
    lane = iota((channels, 128), 1)
    small = jnp.where(lane == 28, dot_nt(dz2, tap_rows), 0.0)
    small = small + jnp.where((lane >= 32) & (lane < 36), dot_nt(h2, tap_rows), 0.0)
    small = small + jnp.where(lane == 29, dot_nt(dpred_tall, tap_rows), 0.0)

    def brick_copy(chunk, act):
        @pl.when(me != chunk)
        def _():
            copy = pltpu.make_async_remote_copy(
                src_ref=rb_src.at[chunk],
                dst_ref=rb_ref.at[me],
                send_sem=b_send.at[chunk],
                recv_sem=b_recv.at[me],
                device_id={"brick": chunk},
                device_id_type=MESH,
            )
            if act == "start":
                copy.start()
            else:
                copy.wait_send()

    mine = pl.ds(pl.multiple_of(mr * rows, rows), rows)

    def region_sum(part):
        lanes = pl.ds(0, MAIN) if part == 0 else pl.ds(MAIN, CHUNK)
        for step in range(nr - 1):
            region_copy(part, step, "recv")
        total = grad_ref[mine, lanes].astype(F32)
        for step in range(nr - 1):
            total = total + ra_ref[(mr + 1 + step) % nr, :, lanes].astype(F32)
        return total

    exchange(2, dz_out, dz_box, "recv")
    padded, halo = widen(dz2.astype(F32), dz_box, flags, spread)
    windows(padded, halo, store_windows(s2_ref))
    dz1 = (convolve(back_ref, s2_ref) * slope1).astype(BF16)
    small = small + jnp.where(lane < 28, dot_nt(dz1, tap_rows), 0.0)
    grad_ref[:, MAIN:] = halves(small)
    for step in range(nr - 1):
        region_copy(1, step, "start")
    total = region_sum(0)
    for chunk in range(CHUNKS - 1):
        rb_src[chunk] = total[:, CHUNK * chunk : CHUNK * (chunk + 1)].astype(BF16)
        brick_copy(chunk, "start")

    def gather_copy(step, act):
        other = (me + 1 + step) % nb
        copy = pltpu.make_async_remote_copy(
            src_ref=fin_ref.at[me % CHUNKS],
            dst_ref=fin_ref.at[me % CHUNKS],
            send_sem=gb_send.at[other],
            recv_sem=gb_recv.at[me % CHUNKS],
            device_id={"brick": other},
            device_id_type=MESH,
        )
        if act == "start":
            copy.start()
        else:
            copy.wait_send()

    def own():
        def arrived(step):
            other = (me + 1 + step) % nb
            pltpu.make_async_remote_copy(
                src_ref=rb_src.at[0],
                dst_ref=rb_ref.at[other],
                send_sem=b_send.at[0],
                recv_sem=b_recv.at[other],
                device_id={"brick": other},
                device_id_type=MESH,
            ).wait_recv()

        for_each(nb - 1, arrived)
        kept = rb_src[me % CHUNKS].astype(F32)
        if nb <= CHUNKS:
            for step in range(nb - 1):
                kept = kept + rb_ref[(me + 1 + step) % nb].astype(F32)
        else:
            kept = lax.fori_loop(
                0, nb - 1, lambda step, s: s + rb_ref[(me + 1 + step) % nb].astype(F32), kept
            )
        fin_ref[me % CHUNKS] = kept.astype(BF16)
        for_each(nb - 1, lambda step: gather_copy(step, "start"))

    def spread_copy(chunk, step, act):
        other = (mr + 1 + step) % nr
        slot_id = other if act == "recv" else mr
        copy = pltpu.make_async_remote_copy(
            src_ref=fin_ref.at[chunk],
            dst_ref=fin_out.at[slot_id, chunk],
            send_sem=ga_send.at[other, chunk],
            recv_sem=ga_recv.at[slot_id, chunk],
            device_id={"region": other},
            device_id_type=MESH,
        )
        if act == "start":
            copy.start()
        elif act == "recv":
            copy.wait_recv()
        else:
            copy.wait_send()

    pl.when(me < CHUNKS - 1)(own)

    def few_copy(step, act):
        other = (me + 1 + step) % nb
        slot_id = other if act == "recv" else me
        copy = pltpu.make_async_remote_copy(
            src_ref=rb_src.at[CHUNKS - 1],
            dst_ref=few_ref.at[slot_id],
            send_sem=few_send.at[other],
            recv_sem=few_recv.at[slot_id],
            device_id={"brick": other},
            device_id_type=MESH,
        )
        if act == "start":
            copy.start()
        elif act == "recv":
            copy.wait_recv()
        else:
            copy.wait_send()

    few = halves(joined(region_sum(1)))
    rb_src[CHUNKS - 1] = few
    for_each(nb - 1, lambda step: few_copy(step, "start"))
    few_ref[me] = few

    def keep(chunk):
        return pltpu.make_async_copy(fin_ref.at[chunk], fin_out.at[mr, chunk], out_sem.at[chunk])

    def pass_on(chunk):
        for step in range(nr - 1):
            spread_copy(chunk, step, "start")
        keep(chunk).start()

    for chunk in range(CHUNKS - 1):
        @pl.when(me != chunk)
        def _():
            pltpu.make_async_remote_copy(
                src_ref=fin_ref.at[chunk],
                dst_ref=fin_ref.at[chunk],
                send_sem=gb_send.at[chunk],
                recv_sem=gb_recv.at[chunk],
                device_id={"brick": chunk},
                device_id_type=MESH,
            ).wait_recv()

        pass_on(chunk)

    for_each(nb - 1, lambda step: few_copy(step, "recv"))
    if nb <= CHUNKS:
        few = joined(few_ref[0])
        for brick in range(1, nb):
            few = few + joined(few_ref[brick])
    else:
        few = lax.fori_loop(1, nb, lambda brick, s: s + joined(few_ref[brick]), joined(few_ref[0]))
    fin_ref[CHUNKS - 1] = halves(few)
    pass_on(CHUNKS - 1)

    exchange(0, mic_out, mic_box, "sent")
    exchange(1, h1_out, h1_box, "sent")
    exchange(2, dz_out, dz_box, "sent")
    for part in range(2):
        for step in range(nr - 1):
            region_copy(part, step, "sent")
    for chunk in range(CHUNKS - 1):
        brick_copy(chunk, "sent")
    pl.when(me < CHUNKS - 1)(lambda: for_each(nb - 1, lambda step: gather_copy(step, "sent")))
    for_each(nb - 1, lambda step: few_copy(step, "sent"))
    pred_copy.wait()
    for chunk in range(CHUNKS):
        keep(chunk).wait()
    for chunk in range(CHUNKS):
        for step in range(nr - 1):
            spread_copy(chunk, step, "recv")
            spread_copy(chunk, step, "sent")


def finish(
    fin_ref, raw_ref, pred_ref, gw1_ref, gb1_ref, gw2_ref, gb2_ref, gwh_ref, gbh_ref
):
    nr, _, rows, _ = fin_ref.shape
    channels = nr * rows
    pred_ref[...] = raw_ref[...]
    for region in range(nr):
        where = slice(region * rows, (region + 1) * rows)
        for chunk in range(CHUNKS - 1):
            block = fin_ref[region, chunk].astype(F32)
            if chunk < CHUNKS - 2:
                gw2_ref[where, CHUNK * chunk : CHUNK * (chunk + 1)] = block
            else:
                gw2_ref[where, CHUNK * chunk : CHUNK * chunk + 128] = block[:, :128]
                gw2_ref[where, CHUNK * chunk + 128 : TAPS * channels] = block[
                    :, 128 : TAPS * channels - CHUNK * chunk
                ]
    small = jnp.concatenate(
        [joined(fin_ref[region, CHUNKS - 1]) for region in range(nr)], axis=0
    )
    turned = jnp.concatenate([small, jnp.zeros((128 - channels, 128), F32)], axis=0).T
    gw1_ref[...] = turned[:TAPS, :channels]
    gb1_ref[...] = turned[27:28, :channels]
    gb2_ref[...] = turned[28:29, :channels]
    gbh_ref[...] = turned[29:30, :4]
    gwh_ref[...] = turned[32:36, :channels]


def solution(mesh):
    nb, nr = mesh.shape["brick"], mesh.shape["region"]

    def shards(mic, tissue, neighbours, w1, b1, w2, b2, hw, hb, cot):
        channels = w1.shape[0]
        rows = channels // nr
        vmem = pl.BlockSpec(memory_space=pltpu.VMEM)
        hbm = pl.BlockSpec(memory_space=pl.ANY)
        smem = pl.BlockSpec(memory_space=pltpu.SMEM)
        dma = pltpu.SemaphoreType.DMA
        total_bricks = nb * nr * mic.shape[1]
        outs = pl.pallas_call(
            functools.partial(kernel, nb, nr, total_bricks),
            out_shape=(
                jax.ShapeDtypeStruct((4, CELLS), BF16),
                jax.ShapeDtypeStruct((nr, CHUNKS, rows, CHUNK), BF16),
            ),
            in_specs=[hbm, smem, smem] + [hbm] * 7,
            out_specs=(hbm,) * 2,
            scratch_shapes=[
                pltpu.VMEM((4, CELLS), BF16),
                pltpu.VMEM((CHUNKS, rows, CHUNK), BF16),
                pltpu.VMEM((nb, rows, CHUNK), BF16),
                pltpu.VMEM((WIDE, WIDE), BF16),
                pltpu.VMEM((WIDE, WIDE), BF16),
                pltpu.VMEM((128, channels), BF16),
                pltpu.VMEM((channels, MAIN), BF16),
                pltpu.VMEM((3 * channels, WIDE), BF16),
                pltpu.VMEM((3 * channels, WIDE), BF16),
                pltpu.VMEM((128, CELLS), BF16),
                pltpu.VMEM((CELLS, 128), BF16),
                pltpu.VMEM((256, WIDE), BF16),
                pltpu.VMEM((2, MIC_ROWS, 128), BF16),
                pltpu.VMEM((2, channels, 128), BF16),
                pltpu.VMEM((2, channels, 128), BF16),
                pltpu.VMEM((6, MIC_ROWS, 128), BF16),
                pltpu.VMEM((6, channels, 128), BF16),
                pltpu.VMEM((6, channels, 128), BF16),
                pltpu.VMEM((channels, MAIN + CHUNK), BF16),
                pltpu.VMEM((nr, rows, MAIN + CHUNK), BF16),
                pltpu.VMEM((CHUNKS, rows, CHUNK), BF16),
                pltpu.VMEM((nb, rows, CHUNK), BF16),
                pltpu.VMEM((1, CELLS), BF16),
                pltpu.VMEM((TAPS, channels), BF16),
                pltpu.VMEM((1, channels), F32),
                pltpu.VMEM((channels, TAPS * channels), BF16),
                pltpu.VMEM((1, channels), F32),
                pltpu.VMEM((4, channels), BF16),
                pltpu.VMEM((1, 4), F32),
                pltpu.VMEM((4, CELLS), BF16),
                dma((8,)),
                dma((CHUNKS + 1,)),
                dma((nb,)),
                dma((nb,)),
                dma((3, 6)),
                dma((3, 6)),
                dma((2, nr)),
                dma((2, nr)),
                dma((CHUNKS,)),
                dma((nb,)),
                dma((nb,)),
                dma((CHUNKS,)),
                dma((nr, CHUNKS)),
                dma((nr, CHUNKS)),
            ],
            compiler_params=pltpu.CompilerParams(
                collective_id=0, has_side_effects=True, vmem_limit_bytes=60 * 1024 * 1024
            ),
            cost_estimate=pl.CostEstimate(flops=360_000_000, bytes_accessed=2_000_000, transcendentals=65536),
        )(
            mic.reshape(1, CELLS),
            tissue,
            neighbours.reshape(1, 26),
            w1.T,
            b1.reshape(1, channels),
            w2,
            b2.reshape(1, channels),
            hw,
            hb.reshape(1, 4),
            cot.reshape(4, CELLS),
        )
        pred, gw1, gb1, gw2, gb2, gwh, gbh = pl.pallas_call(
            finish,
            out_shape=(
                jax.ShapeDtypeStruct((4, CELLS), BF16),
                jax.ShapeDtypeStruct((TAPS, channels), F32),
                jax.ShapeDtypeStruct((1, channels), F32),
                jax.ShapeDtypeStruct((channels, TAPS * channels), F32),
                jax.ShapeDtypeStruct((1, channels), F32),
                jax.ShapeDtypeStruct((4, channels), F32),
                jax.ShapeDtypeStruct((1, 4), F32),
            ),
            in_specs=[vmem] * 2,
            out_specs=(vmem,) * 7,
            compiler_params=pltpu.CompilerParams(vmem_limit_bytes=60 * 1024 * 1024),
        )(outs[1], outs[0])
        return (
            pred.reshape(1, 1, 4, CELLS),
            gw1.T,
            gb1.reshape(channels),
            gw2,
            gb2.reshape(channels),
            gwh,
            gbh.reshape(4),
        )

    return jax.shard_map(
        shards,
        mesh=mesh,
        in_specs=(
            P("region", "brick", None),
            P("region", "brick"),
            P("region", "brick", None),
            P(),
            P(),
            P(),
            P(),
            P(),
            P(),
            P("region", "brick", None, None),
        ),
        out_specs=(P("region", "brick", None, None), P(), P(), P(), P(), P(), P()),
        check_vma=False,
    )
```
